32 devices in a mesh: utt: 16 (over z, x, core), tm: 2 (over y).
Axes of the slice: x: 2, y: 2, z: 4, core: 2. Of those that a mesh axis runs over, the one named last changes fastest.
Arguments:
- noisy_mel: bfloat16 [2, 80, 65536], P('tm', None, 'utt'), may hold values from -6 to 6
- encoder_mean: bfloat16 [80, 65536], P(None, ('utt', 'tm')), may hold values from -6 to 6
- time_embedding: bfloat16 [2, 128, 1024], P('tm', 'utt'), may hold values from -6 to 6
- utter_lengths: int32 [16, 8], P('utt'), may hold values from 1 to 2049, as said below
- out_cotangent: bfloat16 [2, 256, 32768], P('tm', None, 'utt'), may hold values from -6 to 6
- conv_one: bfloat16 [3, 160, 256], replicated, may hold values from -0.25 to 0.25
- bias_one: bfloat16 [256], replicated, may hold values from -3 to 3
- gain_one: bfloat16 [256], replicated, may hold values from 0.099609375 to 1.8984375
- shift_one: bfloat16 [256], replicated, may hold values from -2 to 2
- time_weight: bfloat16 [1024, 256], replicated, may hold values from -0.25 to 0.25
- time_bias: bfloat16 [256], replicated, may hold values from -2 to 2
- conv_two: bfloat16 [3, 256, 256], replicated, may hold values from -0.21875 to 0.21875
- bias_two: bfloat16 [256], replicated, may hold values from -3 to 3
- gain_two: bfloat16 [256], replicated, may hold values from 0.099609375 to 1.8984375
- shift_two: bfloat16 [256], replicated, may hold values from -2 to 2
- skip_weight: bfloat16 [160, 256], replicated, may hold values from -0.5 to 0.5
- skip_bias: bfloat16 [256], replicated, may hold values from -2 to 2
- norm_gain: bfloat16 [256], replicated, may hold values from 0.099609375 to 1.8984375
- norm_shift: bfloat16 [256], replicated, may hold values from -2 to 2
- heads_input: bfloat16 [256, 384], replicated, may hold values from -0.5 to 0.5
- heads_output: bfloat16 [128, 256], replicated, may hold values from -2 to 2
- output_bias: bfloat16 [256], replicated, may hold values from -2 to 2
- feed_gain: bfloat16 [256], replicated, may hold values from 0.099609375 to 1.8984375
- feed_shift: bfloat16 [256], replicated, may hold values from -2 to 2
- expand_weight: bfloat16 [256, 1024], replicated, may hold values from -0.375 to 0.375
- expand_bias: bfloat16 [1024], replicated, may hold values from -2 to 2
- snake_alpha: bfloat16 [1024], replicated, may hold values from 0.5 to 2
- snake_beta: bfloat16 [1024], replicated, may hold values from 0.5 to 2
- reduce_weight: bfloat16 [1024, 256], replicated, may hold values from -0.1875 to 0.1875
- reduce_bias: bfloat16 [256], replicated, may hold values from -2 to 2
- down_weight: bfloat16 [3, 256, 256], replicated, may hold values from -0.21875 to 0.21875
- down_bias: bfloat16 [256], replicated, may hold values from -2 to 2
Outputs:
- down_output: bfloat16 [2, 256, 32768], P('tm', None, 'utt')
- grad_noisy: float32 [2, 80, 65536], P('tm', None, 'utt')
- grad_mean: float32 [80, 65536], P(None, ('utt', 'tm'))
- grad_time: float32 [2, 128, 1024], P('tm', 'utt')
- grad_conv_one: float32 [3, 160, 256], replicated
- grad_bias_one: float32 [256], replicated
- grad_gain_one: float32 [256], replicated
- grad_shift_one: float32 [256], replicated
- grad_time_weight: float32 [1024, 256], replicated
- grad_time_bias: float32 [256], replicated
- grad_conv_two: float32 [3, 256, 256], replicated
- grad_bias_two: float32 [256], replicated
- grad_gain_two: float32 [256], replicated
- grad_shift_two: float32 [256], replicated
- grad_skip_weight: float32 [160, 256], replicated
- grad_skip_bias: float32 [256], replicated
- grad_norm_gain: float32 [256], replicated
- grad_norm_shift: float32 [256], replicated
- grad_heads_input: float32 [256, 384], replicated
- grad_heads_output: float32 [128, 256], replicated
- grad_output_bias: float32 [256], replicated
- grad_feed_gain: float32 [256], replicated
- grad_feed_shift: float32 [256], replicated
- grad_expand_weight: float32 [256, 1024], replicated
- grad_expand_bias: float32 [1024], replicated
- grad_snake_alpha: float32 [1024], replicated
- grad_snake_beta: float32 [1024], replicated
- grad_reduce_weight: float32 [1024, 256], replicated
- grad_reduce_bias: float32 [256], replicated
- grad_down_weight: float32 [3, 256, 256], replicated
- grad_down_bias: float32 [256], replicated
The draws below stay inside these ranges and needn't reach their ends.
Inputs may be any that keep to these rules, and one draw needn't show every extreme that they name: `utter_lengths`: each row lists one index of utt's utterances in the order of their frames; a row's lengths sum to at most 4096, the rest of its frames is padding, and some row sums to exactly 4096. Its longest utterance then has the most frames, which is reached in every draw.
All inputs are finite; a program needn't handle non-finite values.
Results may differ from the reference program's by a relative error of at most 0.025.
The reference program's roundings to bfloat16 on the way count: a program that leaves them out, or rounds other values in their place, can miss the bound.
Values may be sent and summed in bfloat16 or wider, within the bound.
A program may use at most 192 MiB of HBM per device.

```python
import math
import jax
import jax.numpy as jnp
from jax import lax

C_IN = 80
CH = 256
TDIM = 1024
HEADS = 2
HEAD = 64
FFW = 1024
GROUPS = 8
FR_DEV = 4096
SEGS = 8
TIMES = 2
FRAMES = 65536
UTTS = 128
N_UTT = 16


def draw_utter_lengths(key, part):
    key = jax.random.fold_in(key, 11)
    key_pad, key_full, key_share, key_long = jax.random.split(key, 4)
    pad_counts = jax.random.randint(key_pad, (N_UTT,), 0, FR_DEV // 2 + 1)
    full_row = jax.random.randint(key_full, (), 0, N_UTT)
    row_index = jnp.arange(N_UTT)
    pad_counts = jnp.where(row_index == full_row, 0, pad_counts)
    used_frames = FR_DEV - pad_counts
    shares = jax.random.randint(key_share, (N_UTT, SEGS), 1, 9)
    long_place = jax.random.randint(key_long, (N_UTT,), 0, SEGS)
    slot_index = jnp.arange(SEGS)[None, :]
    is_long = slot_index == long_place[:, None]
    shares = jnp.where(is_long, 0, shares)
    share_total = jnp.sum(shares, axis=1)
    budget = FR_DEV // 2 - SEGS
    portions = budget * shares // share_total[:, None]
    portions = jnp.where(is_long, 0, portions)
    remainder = budget - jnp.sum(portions, axis=1)
    filler_place = (long_place + 1) % SEGS
    is_filler = slot_index == filler_place[:, None]
    portions = portions + jnp.where(is_filler, remainder[:, None], 0)
    others = jnp.where(is_long, 0, 1 + portions)
    long_length = used_frames - jnp.sum(others, axis=1)
    lengths_out = jnp.where(is_long, long_length[:, None], others)
    return lengths_out.astype(jnp.int32)


def block_levels(key, dims, cuts, smallest, high):
    gain = 1.0
    for axis_at, blocks in cuts:
        draws = jax.random.uniform(jax.random.fold_in(jax.random.fold_in(key, 6), axis_at), (blocks,), jnp.float32, smallest / len(cuts), high / len(cuts))
        gain = gain * jnp.repeat(jnp.exp(draws), dims[axis_at] // blocks).reshape((-1,) + (1,) * (len(dims) - 1 - axis_at))
    return gain


def centred(rng, dims, scale, bound, pieces=(), held_as=jnp.bfloat16):
    factor_of = block_levels(rng, dims, pieces, -0.22, 0.18) if pieces else 1.0
    array = jax.random.normal(rng, dims, jnp.float32) * scale * factor_of
    return jnp.minimum(jnp.maximum(array, -bound), bound).astype(held_as)


def setup_inputs(seed: int = 0) -> dict:
    splits = jax.random.split(jax.random.key(seed), 33)
    noisy_mel = centred(splits[0], (TIMES, C_IN, FRAMES), 1.0, 6.0, ((0, 2), (2, 16)))
    encoder_mean = centred(splits[1], (C_IN, FRAMES), 1.0, 6.0, ((1, 32),))
    time_embedding = centred(splits[2], (TIMES, UTTS, TDIM), 1.0, 6.0, ((0, 2), (1, 16)))
    utter_lengths = draw_utter_lengths(jax.random.fold_in(splits[32], 71), 0)
    out_cotangent = centred(splits[4], (TIMES, CH, FRAMES // 2), 1.0, 6.0, ((0, 2), (2, 16)))
    conv_one = centred(splits[5], (3, 2 * C_IN, CH), (6 * C_IN) ** -0.5, 0.25)
    bias_one = centred(splits[6], (CH,), 0.5, 3.0)
    gain_one = jnp.clip(1.0 + 0.18 * jax.random.normal(splits[7], (CH,), jnp.float32), 0.099609375, 1.8984375).astype(jnp.bfloat16)
    shift_one = centred(splits[8], (CH,), 0.3, 2.0)
    time_weight = centred(splits[9], (TDIM, CH), (TDIM // 2) ** -0.5, 0.25)
    time_bias = centred(splits[10], (CH,), 0.3, 2.0)
    conv_two = centred(splits[11], (3, CH, CH), (3 * CH) ** -0.5, 0.21875)
    bias_two = centred(splits[12], (CH,), 0.5, 3.0)
    gain_two = jnp.clip(1.0 + 0.18 * jax.random.normal(splits[13], (CH,), jnp.float32), 0.099609375, 1.8984375).astype(jnp.bfloat16)
    shift_two = centred(splits[14], (CH,), 0.3, 2.0)
    skip_weight = centred(splits[15], (2 * C_IN, CH), (2 * C_IN) ** -0.5, 0.5)
    skip_bias = centred(splits[16], (CH,), 0.3, 2.0)
    norm_gain = jnp.clip(1.0 + 0.18 * jax.random.normal(splits[17], (CH,), jnp.float32), 0.099609375, 1.8984375).astype(jnp.bfloat16)
    norm_shift = centred(splits[18], (CH,), 0.3, 2.0)
    heads_input = centred(splits[19], (CH, 3 * HEADS * HEAD), (CH // 2) ** -0.5, 0.5)
    heads_output = centred(splits[20], (HEADS * HEAD, CH), (HEADS * HEAD // 16) ** -0.5, 2.0)
    output_bias = centred(splits[21], (CH,), 0.3, 2.0)
    feed_gain = jnp.clip(1.0 + 0.18 * jax.random.normal(splits[22], (CH,), jnp.float32), 0.099609375, 1.8984375).astype(jnp.bfloat16)
    feed_shift = centred(splits[23], (CH,), 0.3, 2.0)
    expand_weight = centred(splits[24], (CH, FFW), CH ** -0.5, 0.375)
    expand_bias = centred(splits[25], (FFW,), 0.3, 2.0)
    snake_alpha = jnp.clip(jnp.exp(jax.random.uniform(splits[26], (FFW,), jnp.float32, math.log(0.5), math.log(2.0))), 0.5, 2.0).astype(jnp.bfloat16)
    snake_beta = jnp.clip(jnp.exp(jax.random.uniform(splits[27], (FFW,), jnp.float32, math.log(0.5), math.log(2.0))), 0.5, 2.0).astype(jnp.bfloat16)
    reduce_weight = centred(splits[28], (FFW, CH), FFW ** -0.5, 0.1875)
    reduce_bias = centred(splits[29], (CH,), 0.3, 2.0)
    down_weight = centred(splits[30], (3, CH, CH), (3 * CH) ** -0.5, 0.21875)
    down_bias = centred(splits[31], (CH,), 0.3, 2.0)
    return dict(noisy_mel=noisy_mel, encoder_mean=encoder_mean, time_embedding=time_embedding, utter_lengths=utter_lengths, out_cotangent=out_cotangent, conv_one=conv_one, bias_one=bias_one, gain_one=gain_one, shift_one=shift_one, time_weight=time_weight, time_bias=time_bias, conv_two=conv_two, bias_two=bias_two, gain_two=gain_two, shift_two=shift_two, skip_weight=skip_weight, skip_bias=skip_bias, norm_gain=norm_gain, norm_shift=norm_shift, heads_input=heads_input, heads_output=heads_output, output_bias=output_bias, feed_gain=feed_gain, feed_shift=feed_shift, expand_weight=expand_weight, expand_bias=expand_bias, snake_alpha=snake_alpha, snake_beta=snake_beta, reduce_weight=reduce_weight, reduce_bias=reduce_bias, down_weight=down_weight, down_bias=down_bias)


@jax.custom_vjp
def low(v):
    return lax.optimization_barrier(v.astype(jnp.bfloat16)).astype(jnp.float32)

@jax.custom_vjp
def low_back(v):
    return v

def low_keep(v):
    return (low(v), None)

def low_pass(kept, grad):
    return (grad,)

def back_keep(v):
    return (v, None)

def back_low(kept, grad):
    return (low(grad),)
low.defvjp(low_keep, low_pass)
low_back.defvjp(back_keep, back_low)
EPSILON = 1e-05
HIGHEST = lax.Precision.HIGHEST
MASKED = -1e+30

def mish_act(values):
    return values * jnp.tanh(jax.nn.softplus(values))

def pack_layout(lengths_row, frames):
    lengths_row = lengths_row.astype(jnp.int32)
    ends_at = jnp.cumsum(lengths_row).astype(jnp.int32)
    used_frames = ends_at[-1]
    places = jnp.arange(frames, dtype=jnp.int32)
    segment = lax.optimization_barrier(jnp.sum((places[:, None] >= ends_at[None, :]).astype(jnp.int32), axis=1)).astype(jnp.int32)
    onehot = (segment[:, None] == jnp.arange(lengths_row.shape[0], dtype=jnp.int32)[None, :]).astype(jnp.float32)
    frame_mask = (places < used_frames).astype(jnp.float32)
    joined = (segment[1:] == segment[:-1]).astype(jnp.float32)
    zero_one = jnp.zeros((1,), jnp.float32)
    same_prev = jnp.concatenate([zero_one, joined]) * frame_mask
    same_next = jnp.concatenate([joined, zero_one]) * frame_mask
    return (segment, onehot, frame_mask, same_prev, same_next)

def group_norm(pre_act, gain_vec, shift_vec, onehot, counts):
    channels = pre_act.shape[0]
    per_group = channels // GROUPS

    def group_stat(values):
        totals = jnp.dot(values, onehot, precision=HIGHEST)
        grouped = lax.optimization_barrier(jnp.sum(totals.reshape(GROUPS, per_group, -1), axis=1)) / (counts[None, :] * per_group)
        return jnp.repeat(grouped, per_group, axis=0)

    def expand(statistic):
        return jnp.dot(statistic, onehot.T, precision=HIGHEST)
    centered = pre_act - expand(group_stat(pre_act))
    scales = expand(lax.rsqrt(group_stat(centered * centered) + EPSILON))
    return centered * scales * gain_vec[:, None] + shift_vec[:, None]

def layer_norm(values, gain_vec, shift_vec):
    centered = values - lax.optimization_barrier(jnp.mean(values, axis=0, keepdims=True))
    spread = lax.optimization_barrier(jnp.mean(centered * centered, axis=0, keepdims=True))
    return centered * lax.rsqrt(spread + EPSILON) * gain_vec[:, None] + shift_vec[:, None]

def snake_act(values, alpha_vec, beta_vec):
    return values + jnp.sin(alpha_vec[:, None] * values) ** 2 / beta_vec[:, None]

def shift_later(values):
    return jnp.concatenate([jnp.zeros_like(values[:, :1]), values[:, :-1]], axis=1)

def shift_earlier(values):
    return jnp.concatenate([values[:, 1:], jnp.zeros_like(values[:, :1])], axis=1)

def conv_three(weight, inputs, same_prev, same_next):
    before = shift_later(inputs) * same_prev[None]
    after = shift_earlier(inputs) * same_next[None]
    return jnp.dot(weight[0].T, before, precision=HIGHEST) + jnp.dot(weight[1].T, inputs, precision=HIGHEST) + jnp.dot(weight[2].T, after, precision=HIGHEST)

def conv_down(weight, inputs, same_prev, same_next):
    even_cols = inputs[:, 0::2]
    odd_cols = inputs[:, 1::2]
    before = shift_later(odd_cols) * same_prev[0::2][None]
    after = odd_cols * same_next[0::2][None]
    return jnp.dot(weight[0].T, before, precision=HIGHEST) + jnp.dot(weight[1].T, even_cols, precision=HIGHEST) + jnp.dot(weight[2].T, after, precision=HIGHEST)

def pack_forward(noisy_pack, mean_pack, time_pack, lengths_row, params):
    conv_one, bias_one, gain_one, shift_one, time_weight, time_bias, conv_two, bias_two, gain_two, shift_two, skip_weight, skip_bias, norm_gain, norm_shift, heads_input, heads_output, output_bias, feed_gain, feed_shift, expand_weight, expand_bias, snake_alpha, snake_beta, reduce_weight, reduce_bias, down_weight, down_bias = params
    frames = noisy_pack.shape[1]
    segment, onehot, frame_mask, same_prev, same_next = pack_layout(lengths_row, frames)
    counts = lengths_row.astype(jnp.float32)
    inputs = jnp.concatenate([noisy_pack, mean_pack], axis=0) * frame_mask[None]
    pre_one = low_back(conv_three(conv_one, inputs, same_prev, same_next) + bias_one[:, None])
    hidden_one = mish_act(group_norm(pre_one, gain_one, shift_one, onehot, counts)) * frame_mask[None]
    time_proj = low_back(jnp.dot(low(mish_act(time_pack)), time_weight, precision=HIGHEST) + time_bias[None])
    hidden_one = hidden_one + jnp.dot(time_proj.T, onehot.T, precision=HIGHEST)
    act_two = low(hidden_one * frame_mask[None])
    pre_two = low_back(conv_three(conv_two, act_two, same_prev, same_next) + bias_two[:, None])
    hidden_two = mish_act(group_norm(pre_two, gain_two, shift_two, onehot, counts)) * frame_mask[None]
    skip_path = low_back(jnp.dot(skip_weight.T, inputs, precision=HIGHEST) + skip_bias[:, None])
    resid_one = hidden_two + skip_path
    normed_one = low(layer_norm(resid_one, norm_gain, norm_shift))
    projected = low_back(low(jnp.dot(heads_input.T, normed_one, precision=HIGHEST)))
    inner = heads_output.shape[0]
    head_size = inner // HEADS
    queries = projected[:inner].reshape(HEADS, head_size, frames)
    keys_all = projected[inner:2 * inner].reshape(HEADS, head_size, frames)
    values_all = projected[2 * inner:].reshape(HEADS, head_size, frames)
    scores = low_back(jnp.einsum('hdq,hdk->hqk', queries, keys_all, precision=HIGHEST) * head_size ** (-0.5))
    allowed = (segment[:, None] == segment[None, :])[None]
    scores = jnp.where(allowed, scores, MASKED)
    weights = low(jax.nn.softmax(scores, axis=-1))
    attended = jnp.einsum('hqk,hdk->hdq', weights, values_all, precision=HIGHEST).reshape(inner, frames)
    attended = low_back(low(attended))
    attn_path = low_back(jnp.dot(heads_output.T, attended, precision=HIGHEST) + output_bias[:, None])
    resid_two = resid_one + attn_path
    normed_two = low(layer_norm(resid_two, feed_gain, feed_shift))
    expanded = low_back(jnp.dot(expand_weight.T, normed_two, precision=HIGHEST) + expand_bias[:, None])
    snaked = low(snake_act(expanded, snake_alpha, snake_beta))
    reduced = low_back(jnp.dot(reduce_weight.T, snaked, precision=HIGHEST) + reduce_bias[:, None])
    resid_three = resid_two + reduced
    down_in = low(resid_three * frame_mask[None])
    down_pre = conv_down(down_weight, down_in, same_prev, same_next) + down_bias[:, None]
    return down_pre * frame_mask[0::2][None]

def reference(noisy_mel, encoder_mean, time_embedding, utter_lengths, out_cotangent, conv_one, bias_one, gain_one, shift_one, time_weight, time_bias, conv_two, bias_two, gain_two, shift_two, skip_weight, skip_bias, norm_gain, norm_shift, heads_input, heads_output, output_bias, feed_gain, feed_shift, expand_weight, expand_bias, snake_alpha, snake_beta, reduce_weight, reduce_bias, down_weight, down_bias):
    weights_in = (conv_one, bias_one, gain_one, shift_one, time_weight, time_bias, conv_two, bias_two, gain_two, shift_two, skip_weight, skip_bias, norm_gain, norm_shift, heads_input, heads_output, output_bias, feed_gain, feed_shift, expand_weight, expand_bias, snake_alpha, snake_beta, reduce_weight, reduce_bias, down_weight, down_bias)
    params_in = tuple((item.astype(jnp.float32) for item in weights_in))
    lengths_all = jnp.broadcast_to(utter_lengths.astype(jnp.int32)[None], (TIMES, N_UTT, SEGS)).reshape(TIMES * N_UTT, SEGS)

    def forward(noisy_all, mean_all, time_all, *params):
        noisy_packs = noisy_all.reshape(TIMES, C_IN, N_UTT, FR_DEV).transpose(0, 2, 1, 3).reshape(TIMES * N_UTT, C_IN, FR_DEV)
        mean_packs = mean_all.reshape(C_IN, N_UTT, FR_DEV).transpose(1, 0, 2)
        mean_packs = jnp.broadcast_to(mean_packs[None], (TIMES, N_UTT, C_IN, FR_DEV)).reshape(TIMES * N_UTT, C_IN, FR_DEV)
        time_packs = time_all.reshape(TIMES * N_UTT, SEGS, TDIM)

        def one_pack(item):
            return pack_forward(item[0], item[1], item[2], item[3], params)
        results = lax.map(jax.checkpoint(one_pack), (noisy_packs, mean_packs, time_packs, lengths_all))
        results = results.reshape(TIMES, N_UTT, CH, FR_DEV // 2).transpose(0, 2, 1, 3)
        return results.reshape(TIMES, CH, N_UTT * (FR_DEV // 2))
    primal, pullback = jax.vjp(forward, noisy_mel.astype(jnp.float32), encoder_mean.astype(jnp.float32), time_embedding.astype(jnp.float32), *params_in)
    grads = pullback(out_cotangent.astype(jnp.float32))
    return (primal.astype(jnp.bfloat16), grads[0], grads[1], grads[2], grads[3], grads[4], grads[5], grads[6], grads[7], grads[8], grads[9], grads[10], grads[11], grads[12], grads[13], grads[14], grads[15], grads[16], grads[17], grads[18], grads[19], grads[20], grads[21], grads[22], grads[23], grads[24], grads[25], grads[26], grads[27], grads[28], grads[29])
```

```python
import functools

import jax
import jax.numpy as jnp
import numpy as np
from jax import lax
from jax.experimental import pallas as pl
from jax.experimental.pallas import tpu as pltpu
from jax.sharding import PartitionSpec as P

GROUPS = 8
EPSILON = 1e-05
BIG = 1e30
TILE = 256


def split_three(row):
    top = row.astype(jnp.bfloat16)
    rest = row - top.astype(jnp.float32)
    mid = rest.astype(jnp.bfloat16)
    last = (rest - mid.astype(jnp.float32)).astype(jnp.bfloat16)
    return (top, mid, last)


def segment_of(places, lens_ref, segs):
    segment = jnp.zeros(places.shape, jnp.int32)
    end = jnp.int32(0)
    for index in range(segs):
        end = end + lens_ref[index]
        segment = segment + (places >= end).astype(jnp.int32)
    return segment


def used_of(lens_ref, segs):
    total = jnp.int32(0)
    for index in range(segs):
        total = total + lens_ref[index]
    return total


def key_bounds(first, used, lens_ref, segs):
    last = jnp.minimum(first + TILE, used) - 1
    low = jnp.int32(0)
    high = used
    end = jnp.int32(0)
    for index in range(segs):
        start = end
        end = end + lens_ref[index]
        low = jnp.where(start <= first, start, low)
        high = jnp.where((start <= last) & (last < end), end, high)
    high = jnp.where(first + TILE > used, first + TILE, high)
    low = low // 128 * 128
    return (low, (high - low + TILE - 1) // TILE)


def fill_keys(kx_ref, rows_ref, row_at, lens_ref, segs, tail):
    tiles = rows_ref.shape[1] // TILE

    def step(index, carry):
        at = pl.multiple_of(index * TILE, TILE)
        source = pl.multiple_of(jnp.minimum(index, tiles - 1) * TILE, TILE)
        rows = rows_ref[row_at : row_at + 128, pl.ds(source, TILE)].astype(jnp.float32)
        rows = jnp.where(index < tiles, rows, 0.0)
        kx_ref[pl.ds(at, TILE), 0:128] = rows.T.astype(jnp.bfloat16)
        lane = lax.broadcasted_iota(jnp.int32, (TILE, 128), 1)
        if tail == "segments":
            place = lax.broadcasted_iota(jnp.int32, (TILE, 128), 0) + at
            segment = segment_of(place, lens_ref, segs)
            hot = (lane == segment) | ((lane >= 16) & (lane < 19))
        else:
            hot = lane < 3
        kx_ref[pl.ds(at, TILE), 128:256] = hot.astype(jnp.float32).astype(jnp.bfloat16)
        return carry

    lax.fori_loop(0, tiles + 1, step, 0)


def copy_padded(padded_ref, rows_ref, row_at):
    frames = rows_ref.shape[1]
    padded_ref[:, 0:frames] = rows_ref[row_at : row_at + 128, :]
    padded_ref[:, frames : frames + TILE] = jnp.zeros((128, TILE), padded_ref.dtype)


def query_tail(first, lens_ref, segs):
    row = lax.broadcasted_iota(jnp.int32, (16, TILE), 0)
    place = lax.broadcasted_iota(jnp.int32, (16, TILE), 1) + first
    segment = segment_of(place, lens_ref, segs)
    return jnp.where(row == segment, 0.0, -BIG).astype(jnp.bfloat16)


def three_rows(row):
    top, mid, last = split_three(row)
    at = lax.broadcasted_iota(jnp.int32, (16, row.shape[1]), 0)
    parts = jnp.where(
        at == 0,
        top.astype(jnp.float32),
        jnp.where(at == 1, mid.astype(jnp.float32), jnp.where(at == 2, last.astype(jnp.float32), 0.0)),
    )
    return parts.astype(jnp.bfloat16)


def fold_heads(rows, extra_one, extra_two):
    blank = jnp.zeros((64, TILE), jnp.bfloat16)
    fill_one = jnp.zeros((128 - extra_one.shape[0], TILE), jnp.bfloat16)
    left = jnp.concatenate([rows[0:64], blank, extra_one, fill_one], axis=0)
    right = jnp.concatenate([blank, rows[64:128], extra_two, fill_one], axis=0)
    return jnp.concatenate([left, right], axis=1)


def row_eights(values):
    return values.reshape(values.shape[0] // 8, 8, values.shape[1])


def by_tiles(widths, low, tiles, step, state):
    done = jnp.int32(0)
    for width in widths:
        end = done + (tiles - done) // width

        def wide_step(index, carry, width=width, start=done):
            place = start + (index - start) * width
            return step(pl.multiple_of(low + place * TILE, 128), width * TILE, place, carry)

        state = lax.fori_loop(done, end, wide_step, state)
        done = done + (end - done) * width
    return state


def scores_are_small(proj_ref):
    within = jnp.bool_(True)
    for head in range(2):
        norms = []
        for at in (64 * head, 128 + 64 * head):
            rows = proj_ref[at : at + 64, :].astype(jnp.float32)
            norms.append(jnp.max(jnp.sum(rows * rows, axis=0, keepdims=True)))
        within = within & (norms[0] * norms[1] <= 480.0 * 480.0)
    return within


def attn_forward_kernel(segs, lens_ref, proj_ref, att_ref, lse_ref, kx_ref, v_ref, score_ref):
    used = used_of(lens_ref, segs)
    small = scores_are_small(proj_ref)
    count = (used + TILE - 1) // TILE
    fill_keys(kx_ref, proj_ref, 128, lens_ref, segs, "segments")
    copy_padded(v_ref, proj_ref, 256)
    att_ref[...] = jnp.zeros_like(att_ref)
    lse_ref[...] = jnp.zeros_like(lse_ref)

    def query_step(index, carry):
        first = pl.multiple_of(index * TILE, TILE)
        queries = proj_ref[0:128, pl.ds(first, TILE)] * jnp.bfloat16(0.125)
        tail = query_tail(first, lens_ref, segs)
        folded = fold_heads(queries, tail, tail)
        low, tiles = key_bounds(first, used, lens_ref, segs)

        def score_step(at, width, place, top):
            scores = jnp.dot(kx_ref[pl.ds(at, width), :], folded, preferred_element_type=jnp.float32)
            score_ref[pl.ds(pl.multiple_of(place * TILE, TILE), width), :] = scores
            return jnp.maximum(top, jnp.max(row_eights(scores), axis=0))

        start = (
            jnp.zeros((8, 2 * TILE), jnp.float32),
            jnp.zeros((64, TILE), jnp.float32),
            jnp.zeros((64, TILE), jnp.float32),
        )

        def weigh(probs, at, state):
            total, one, two = state
            total = total + jnp.sum(row_eights(probs), axis=0)
            low_probs = probs.astype(jnp.bfloat16)
            one = one + jnp.dot(
                v_ref[0:64, pl.ds(at, TILE)], low_probs[:, 0:TILE], preferred_element_type=jnp.float32
            )
            two = two + jnp.dot(
                v_ref[64:128, pl.ds(at, TILE)], low_probs[:, TILE:], preferred_element_type=jnp.float32
            )
            return (total, one, two)

        def direct_step(at, width, place, state):
            scores = jnp.dot(kx_ref[pl.ds(at, width), :], folded, preferred_element_type=jnp.float32)
            for piece in range(0, width, TILE):
                state = weigh(jnp.exp(scores[piece : piece + TILE]), pl.multiple_of(at + piece, 128), state)
            return state

        def with_top():
            top = by_tiles((2, 1), low, tiles, score_step, jnp.full((8, 2 * TILE), -2.0 * BIG, jnp.float32))
            top = jnp.max(top, axis=0, keepdims=True)

            def value_step(at, width, place, state):
                scores = score_ref[pl.ds(pl.multiple_of(place * TILE, TILE), width), :]
                return weigh(jnp.exp(scores - top), at, state)

            return (top,) + by_tiles((1,), low, tiles, value_step, start)

        def without_top():
            return (jnp.zeros((1, 2 * TILE), jnp.float32),) + by_tiles((4, 2, 1), low, tiles, direct_step, start)

        top, total, one, two = lax.cond(small, without_top, with_top)
        total = jnp.sum(total, axis=0, keepdims=True)
        inverse = 1.0 / total
        att_ref[0:64, pl.ds(first, TILE)] = one * inverse[:, 0:TILE]
        att_ref[64:128, pl.ds(first, TILE)] = two * inverse[:, TILE:]
        lse = top + jnp.log(total)
        lse_ref[0:1, pl.ds(first, TILE)] = lse[:, 0:TILE]
        lse_ref[1:2, pl.ds(first, TILE)] = lse[:, TILE:]
        return carry

    lax.fori_loop(0, count, query_step, 0)


def attn_backward_kernel(
    segs, lens_ref, proj_ref, att_ref, lse_ref, gatt_ref, out_ref, kx_ref, vx_ref, k_ref, sums_ref
):
    used = used_of(lens_ref, segs)
    count = (used + TILE - 1) // TILE
    fill_keys(kx_ref, proj_ref, 128, lens_ref, segs, "segments")
    fill_keys(vx_ref, proj_ref, 256, lens_ref, segs, "ones")
    copy_padded(k_ref, proj_ref, 128)
    out_ref[...] = jnp.zeros_like(out_ref)
    sums_ref[...] = jnp.zeros_like(sums_ref)

    def query_step(index, carry):
        first = pl.multiple_of(index * TILE, TILE)
        queries = proj_ref[0:128, pl.ds(first, TILE)] * jnp.bfloat16(0.125)
        tail = query_tail(first, lens_ref, segs)
        lse_one = three_rows(-lse_ref[0:1, pl.ds(first, TILE)])
        lse_two = three_rows(-lse_ref[1:2, pl.ds(first, TILE)])
        folded = fold_heads(
            queries, jnp.concatenate([tail, lse_one], axis=0), jnp.concatenate([tail, lse_two], axis=0)
        )
        grads = gatt_ref[:, pl.ds(first, TILE)]
        weighted = grads.astype(jnp.float32) * att_ref[:, pl.ds(first, TILE)]
        delta_one = three_rows(-jnp.sum(weighted[0:64], axis=0, keepdims=True))
        delta_two = three_rows(-jnp.sum(weighted[64:128], axis=0, keepdims=True))
        grad_folded = fold_heads(grads, delta_one, delta_two)
        low, tiles = key_bounds(first, used, lens_ref, segs)
        transposed = (((1,), (1,)), ((), ()))

        def key_step(at, width, place, state):
            one, two = state

            def spot(piece):
                return pl.ds(pl.multiple_of(at + piece, 128), TILE)

            scores = jnp.dot(kx_ref[pl.ds(at, width), :], folded, preferred_element_type=jnp.float32)
            pulled = jnp.dot(vx_ref[pl.ds(at, width), :], grad_folded, preferred_element_type=jnp.float32)
            for piece in range(0, width, TILE):
                probs = jnp.exp(scores[piece : piece + TILE])
                score_grads = (probs * pulled[piece : piece + TILE]).astype(jnp.bfloat16)
                low_probs = probs.astype(jnp.bfloat16)
                sums_ref[0:128, spot(piece)] += lax.dot_general(
                    folded[0:128], score_grads, transposed, preferred_element_type=jnp.float32
                )
                sums_ref[128:256, spot(piece)] += lax.dot_general(
                    grad_folded[0:128], low_probs, transposed, preferred_element_type=jnp.float32
                )
                one = one + jnp.dot(
                    k_ref[0:64, spot(piece)], score_grads[:, 0:TILE], preferred_element_type=jnp.float32
                )
                two = two + jnp.dot(
                    k_ref[64:128, spot(piece)], score_grads[:, TILE:], preferred_element_type=jnp.float32
                )
            return (one, two)

        blank = jnp.zeros((64, TILE), jnp.float32)
        one, two = by_tiles((4, 2, 1), low, tiles, key_step, (blank, blank))
        out_ref[0:64, pl.ds(first, TILE)] = (one * 0.125).astype(jnp.bfloat16)
        out_ref[64:128, pl.ds(first, TILE)] = (two * 0.125).astype(jnp.bfloat16)
        return carry

    lax.fori_loop(0, count, query_step, 0)

    def write_step(index, carry):
        at = pl.multiple_of(index * TILE, TILE)
        out_ref[128:384, pl.ds(at, TILE)] = sums_ref[:, pl.ds(at, TILE)].astype(jnp.bfloat16)
        return carry

    lax.fori_loop(0, count, write_step, 0)


VMEM_LIMIT = 62 * 1024 * 1024
WHOLE = pl.BlockSpec(memory_space=pltpu.VMEM)
SCALARS = pl.BlockSpec(memory_space=pltpu.SMEM)
ANYWHERE = pl.BlockSpec(memory_space=pl.ANY)
PARAMS = pltpu.CompilerParams(vmem_limit_bytes=VMEM_LIMIT)


def attention_forward(projected, lengths_row):
    frames = projected.shape[1]
    segs = lengths_row.shape[0]
    return pl.pallas_call(
        functools.partial(attn_forward_kernel, segs),
        name="attention_forward",
        out_shape=(
            jax.ShapeDtypeStruct((128, frames), jnp.float32),
            jax.ShapeDtypeStruct((8, frames), jnp.float32),
        ),
        in_specs=[SCALARS, WHOLE],
        out_specs=(WHOLE, WHOLE),
        scratch_shapes=[
            pltpu.VMEM((frames + TILE, 256), jnp.bfloat16),
            pltpu.VMEM((128, frames + TILE), jnp.bfloat16),
            pltpu.VMEM((frames + TILE, 2 * TILE), jnp.float32),
        ],
        compiler_params=PARAMS,
    )(lengths_row, projected)


def attention_backward(projected, attended, log_sums, grad_attended, lengths_row):
    frames = projected.shape[1]
    segs = lengths_row.shape[0]
    return pl.pallas_call(
        functools.partial(attn_backward_kernel, segs),
        name="attention_backward",
        out_shape=jax.ShapeDtypeStruct((384, frames), jnp.bfloat16),
        in_specs=[SCALARS, WHOLE, WHOLE, WHOLE, WHOLE],
        out_specs=WHOLE,
        scratch_shapes=[
            pltpu.VMEM((frames + TILE, 256), jnp.bfloat16),
            pltpu.VMEM((frames + TILE, 256), jnp.bfloat16),
            pltpu.VMEM((128, frames + TILE), jnp.bfloat16),
            pltpu.VMEM((256, frames + TILE), jnp.float32),
        ],
        compiler_params=PARAMS,
        cost_estimate=pl.CostEstimate(flops=40_000_000_000, bytes_accessed=10_000_000, transcendentals=0),
    )(lengths_row, projected, attended, log_sums, grad_attended)


NT = (((1,), (1,)), ((), ()))


def dot(left, right):
    return jnp.dot(left, right, preferred_element_type=jnp.float32)


def dot_nt(left, right):
    return lax.dot_general(left, right, NT, preferred_element_type=jnp.float32)


def places_of(first, width):
    return lax.broadcasted_iota(jnp.int32, (1, width), 1) + first


def frame_masks(places, lens_ref, segs):
    used = used_of(lens_ref, segs)
    here = segment_of(places, lens_ref, segs)
    before = segment_of(places - 1, lens_ref, segs)
    after = segment_of(places + 1, lens_ref, segs)
    valid = places < used
    prev = valid & (here == before) & (places > 0)
    succ = valid & (here == after)
    return (valid.astype(jnp.float32), prev.astype(jnp.float32), succ.astype(jnp.float32))


def plane_of(utts, times):
    rest = utts // 2
    far = 4 if rest % 4 == 0 else 1
    near = rest // far
    return (near, far, near * times * 2)


def block_lanes(index, width):
    return pl.ds(pl.multiple_of(index * width, width), width)


def vector_row(ref):
    return ref[...].astype(jnp.float32).reshape(1, -1)


def vector_columns(refs, cols_ref):
    rows = [vector_row(ref) for ref in refs]
    rows.append(jnp.zeros((cols_ref.shape[1] - len(rows), rows[0].shape[1]), jnp.float32))
    cols_ref[...] = jnp.concatenate(rows, axis=0).T


def lane_fold(values):
    out = values[:, 0:128]
    for at in range(128, values.shape[1], 128):
        out = out + values[:, at : at + 128]
    return out


def column_sums(partial_ref):
    return jnp.sum(partial_ref[...].T, axis=0, keepdims=True)


def norm_frames(values):
    mean = jnp.mean(values, axis=0, keepdims=True)
    centered = values - mean
    spread = jnp.mean(centered * centered, axis=0, keepdims=True)
    scale = lax.rsqrt(spread + EPSILON)
    return (centered * scale, scale)


def norm_frames_back(grad_hat, hat, scale):
    mean_one = jnp.mean(grad_hat, axis=0, keepdims=True)
    mean_two = jnp.mean(grad_hat * hat, axis=0, keepdims=True)
    return scale * (grad_hat - mean_one - hat * mean_two)


BLOCK = 512
RES_BLOCK = 1024
PI = 3.141592653589793


def fit_even(function, terms):
    points = 0.25 * (1.0 - np.cos(np.pi * (np.arange(400) + 0.5) / 400))
    roots = np.sqrt(points)
    basis = np.polynomial.chebyshev.chebvander(8.0 * points - 1.0, terms - 1)
    fitted = np.linalg.lstsq(basis, function(roots), rcond=None)[0]
    series = np.polynomial.chebyshev.Chebyshev(fitted, domain=[0.0, 0.25])
    return [float(item) for item in series.convert(kind=np.polynomial.Polynomial).coef]


SIN_OVER = fit_even(lambda f: np.sin(PI * f) / f, 5)
ROUNDER = 1.5 * 2.0**23


def horner(coefficients, values):
    out = coefficients[-1]
    for item in coefficients[-2::-1]:
        out = out * values + item
    return out


def ffn_kernel(segs, utts, times, lens_ref, *refs):
    near, far, group = plane_of(utts, times)
    chips = group // 2
    ffn_body(segs, lens_ref, refs[0:5], refs[5:8], *refs[8:18], *refs[18 + chips :])
    pack_ref = refs[18 + chips]
    spot = lax.axis_index("utt") // 2 % near * times + lax.axis_index("tm")
    rows = pack_ref.shape[0] // group
    for step in range(chips):
        other = (spot + step) % chips
        for core in range(2):
            at = pl.multiple_of((core * chips + other) * rows, 16)
            refs[18 + step][core * rows : core * rows + rows, :] = pack_ref[pl.ds(at, rows), :]


def chunk_moves(utts, times, step):
    near, far, group = plane_of(utts, times)
    chips = group // 2
    moves = []
    for z in range(far):
        for core in range(2):
            for spot in range(chips):
                ends = []
                for place in (spot, (spot + step) % chips):
                    ends.append((((z * near + place // times) * 2 + core) * times) + place % times)
                moves.append(tuple(ends))
    return moves


def ffn_body(
    segs,
    lens_ref,
    vecs,
    wides,
    resid_hbm,
    att_hbm,
    cot_ref,
    wo_ref,
    we_ref,
    wr_ref,
    wd_ref,
    down_hbm,
    gtwo_hbm,
    gatt_hbm,
    pack_ref,
    gwd_ref,
    gwr_ref,
    gwe_ref,
    gwo_ref,
    cols_ref,
    wide_cols_ref,
    wo_t,
    we_t,
    wr_t,
    wd_t,
    part_ref,
    wide_part_ref,
    odd_ref,
    snaked_ref,
    gexp_ref,
    expand_ref,
    pull_ref,
    resid_ref,
    att_ref,
    down_ref,
    gtwo_ref,
    gatt_ref,
    copy_sem,
):
    frames = resid_ref.shape[1]
    half = BLOCK // 2
    moved = (
        (resid_hbm, resid_ref, BLOCK), (att_hbm, att_ref, BLOCK), (down_ref, down_hbm, half),
        (gtwo_ref, gtwo_hbm, BLOCK), (gatt_ref, gatt_hbm, BLOCK),
    )

    def move(which, index):
        source, target, width = moved[which]
        lanes = block_lanes(index, width)
        return pltpu.make_async_copy(source.at[:, lanes], target.at[:, lanes], copy_sem.at[which, index])

    for index in range(frames // BLOCK):
        move(0, index).start()
        move(1, index).start()
    vector_columns(vecs, cols_ref)
    vector_columns(wides, wide_cols_ref)
    wide_cols_ref[:, 3:4] = wide_cols_ref[:, 1:2] * (1.0 / PI)
    wide_cols_ref[:, 2:3] = 1.0 / wide_cols_ref[:, 2:3]
    wide_cols_ref[:, 4:5] = 2.0 * wide_cols_ref[:, 1:2] * wide_cols_ref[:, 2:3]
    wo_t[...] = wo_ref[...].T
    we_t[...] = we_ref[...].T
    wr_t[...] = wr_ref[...].T
    for tap in range(3):
        wd_t[tap] = wd_ref[tap].T
    for ref in (gwd_ref, gwr_ref, gwe_ref, gwo_ref, part_ref, wide_part_ref, odd_ref):
        ref[...] = jnp.zeros_like(ref)
    row_at = lax.broadcasted_iota(jnp.int32, (256, 256), 0)
    lane_at = lax.broadcasted_iota(jnp.int32, (256, 256), 1)
    source = jnp.where(lane_at < 128, 2 * lane_at, 2 * lane_at - 255)
    gather = (row_at == source).astype(jnp.float32).astype(jnp.bfloat16)
    row_half = lax.broadcasted_iota(jnp.int32, (128, 256), 0)
    lane_half = lax.broadcasted_iota(jnp.int32, (128, 256), 1)
    put_even = (lane_half == 2 * row_half).astype(jnp.float32).astype(jnp.bfloat16)
    put_odd = (lane_half == 2 * row_half + 1).astype(jnp.float32).astype(jnp.bfloat16)

    def column(index):
        return cols_ref[:, index : index + 1]

    def block_step(index, carry):
        first = pl.multiple_of(index * BLOCK, BLOCK)
        first_half = pl.multiple_of(index * half, half)
        valid, _, _ = frame_masks(places_of(first, BLOCK), lens_ref, segs)
        even_places = 2 * places_of(first_half, half + 128)
        even_valid, even_prev, even_next = frame_masks(even_places, lens_ref, segs)
        cot_here = cot_ref[:, pl.ds(first_half, half)].astype(jnp.float32) * even_valid[:, 0:half]
        after_at = pl.multiple_of(jnp.minimum(first_half + half, frames // 2 - 128), 128)
        cot_after = cot_ref[:, pl.ds(after_at, 128)].astype(jnp.float32)
        g_down = cot_here.astype(jnp.bfloat16)
        with_prev = jnp.concatenate([cot_here, cot_after], axis=1) * even_prev
        from_next = pltpu.roll(with_prev, half + 127, 1)[:, 0:half].astype(jnp.bfloat16)
        to_next = (cot_here * even_next[:, 0:half]).astype(jnp.bfloat16)
        thirds = []
        for at in range(0, half, 128):
            spread_even = dot(g_down[:, at : at + 128], put_even).astype(jnp.bfloat16)
            spread_next = dot(to_next[:, at : at + 128], put_odd).astype(jnp.bfloat16)
            spread_prev = dot(from_next[:, at : at + 128], put_odd).astype(jnp.bfloat16)
            thirds.append(
                dot(wd_ref[1], spread_even) + dot(wd_ref[2], spread_next) + dot(wd_ref[0], spread_prev)
            )
        g_three = jnp.concatenate(thirds, axis=1) * valid
        g_reduce = g_three.astype(jnp.bfloat16)
        part_ref[0] += lane_fold(cot_here)
        part_ref[1] += lane_fold(g_reduce.astype(jnp.float32))
        move(0, index).wait()
        move(1, index).wait()
        att_low = att_ref[:, pl.ds(first, BLOCK)].astype(jnp.bfloat16)
        resid_two = resid_ref[:, pl.ds(first, BLOCK)] + dot(wo_t[...], att_low) + column(0)
        hat, scale = norm_frames(resid_two)
        normed = (hat * column(1) + column(2)).astype(jnp.bfloat16)
        expand_ref[...] = dot(we_t[...], normed)
        pull_ref[...] = dot(wr_ref[...], g_reduce)
        for row in range(0, wr_ref.shape[0], 32):
            span = slice(row, row + 32)
            values = expand_ref[span, :] + wide_cols_ref[span, 0:1]
            turns = values * wide_cols_ref[span, 3:4]
            turns = turns - ((turns + ROUNDER) - ROUNDER)
            sine = horner(SIN_OVER, turns * turns) * turns
            sine_two = sine * sine
            cosine_two = jnp.maximum(1.0 - sine_two, 1e-12)
            double = sine * (cosine_two * lax.rsqrt(cosine_two))
            snaked_ref[span, :] = (values + sine_two * wide_cols_ref[span, 2:3]).astype(jnp.bfloat16)
            pulled = pull_ref[span, :]
            slope = pulled * double
            grown = pulled + slope * wide_cols_ref[span, 4:5]
            gexp_ref[span, :] = grown.astype(jnp.bfloat16)
            wide_part_ref[0, span, :] += lane_fold(slope * values)
            wide_part_ref[1, span, :] += lane_fold(pulled * sine_two)
            wide_part_ref[2, span, :] += lane_fold(grown)
        gwr_ref[...] += dot_nt(snaked_ref[...], g_reduce)
        gwe_ref[...] += dot_nt(gexp_ref[...], normed)
        reduced = dot(wr_t[...], snaked_ref[...])
        g_normed = dot(we_ref[...], gexp_ref[...])
        down_in = ((resid_two + reduced + column(3)) * valid).astype(jnp.bfloat16)
        evens = []
        odds = []
        for at in range(0, BLOCK, 256):
            both = dot(down_in[:, at : at + 256], gather)
            evens.append(both[:, 0:128])
            odds.append(both[:, 128:256])
        even_low = jnp.concatenate(evens, axis=1).astype(jnp.bfloat16)
        odd = jnp.concatenate(odds, axis=1)
        led = jnp.concatenate([odd_ref[...], odd], axis=1)
        odd_ref[...] = odd[:, half - 128 : half]
        before = (pltpu.roll(led, 1, 1)[:, 128:] * even_prev[:, 0:half]).astype(jnp.bfloat16)
        after = (odd * even_next[:, 0:half]).astype(jnp.bfloat16)
        down_pre = dot(wd_t[0], before) + dot(wd_t[1], even_low) + dot(wd_t[2], after) + column(4)
        down_ref[:, pl.ds(first_half, half)] = (down_pre * even_valid[:, 0:half]).astype(jnp.bfloat16)
        gwd_ref[0] += dot_nt(before, g_down)
        gwd_ref[1] += dot_nt(even_low, g_down)
        gwd_ref[2] += dot_nt(after, g_down)
        part_ref[2] += lane_fold(g_normed * hat)
        part_ref[3] += lane_fold(g_normed)
        g_two = g_three + norm_frames_back(g_normed * column(1), hat, scale)
        gtwo_ref[:, pl.ds(first, BLOCK)] = g_two
        g_attn = g_two.astype(jnp.bfloat16)
        part_ref[4] += lane_fold(g_attn.astype(jnp.float32))
        gwo_ref[...] += dot_nt(att_low, g_attn)
        gatt_ref[:, pl.ds(first, BLOCK)] = dot(wo_ref[...], g_attn).astype(jnp.bfloat16)
        for which in range(2, 5):
            move(which, index).start()
        return carry

    lax.fori_loop(0, frames // BLOCK, block_step, 0)
    over_beta_row = 1.0 / vector_row(wides[2])
    wide_rows = (
        column_sums(wide_part_ref.at[2]),
        column_sums(wide_part_ref.at[0]) * (2.0 * over_beta_row),
        -column_sums(wide_part_ref.at[1]) * (over_beta_row * over_beta_row),
    )
    rows = [column_sums(part_ref.at[index]) for index in range(5)]
    rows.extend(row[:, at : at + 256] for row in wide_rows for at in range(0, 1024, 256))
    rows.append(jnp.zeros((15, 256), jnp.float32))
    for tap in range(3):
        pack_ref[256 * tap : 256 * tap + 256, :] = gwd_ref[tap].astype(jnp.bfloat16)
    pack_ref[768:1792, :] = gwr_ref[...].astype(jnp.bfloat16)
    pack_ref[1792:2816, :] = gwe_ref[...].astype(jnp.bfloat16)
    pack_ref[2816:2944, :] = gwo_ref[...].astype(jnp.bfloat16)
    pack_ref[2944:2976, :] = jnp.concatenate(rows, axis=0).astype(jnp.bfloat16)
    for which in range(2, 5):
        for index in range(frames // BLOCK):
            move(which, index).wait()
    if pack_ref.shape[0] > 2976:
        pack_ref[2976:, :] = jnp.zeros((pack_ref.shape[0] - 2976, 256), jnp.bfloat16)


def feed_forward(utts, times, pack_rows, lengths_row, vecs, wides, resid_one, attended, cot, wo, we, wr, wd):
    frames = resid_one.shape[1]
    chunks = plane_of(utts, times)[2] // 2
    f32 = jnp.float32
    bf16 = jnp.bfloat16
    return pl.pallas_call(
        functools.partial(ffn_kernel, lengths_row.shape[0], utts, times),
        name="feed_forward",
        out_shape=(
            jax.ShapeDtypeStruct((256, frames // 2), bf16),
            jax.ShapeDtypeStruct((256, frames), f32),
            jax.ShapeDtypeStruct((128, frames), bf16),
        )
        + (jax.ShapeDtypeStruct((pack_rows // chunks, 256), bf16),) * chunks,
        in_specs=[SCALARS] + [WHOLE] * 8 + [ANYWHERE] * 2 + [WHOLE] * 5,
        out_specs=(ANYWHERE,) * 3 + (WHOLE,) * chunks,
        scratch_shapes=[
            pltpu.VMEM((pack_rows, 256), bf16),
            pltpu.VMEM((3, 256, 256), f32),
            pltpu.VMEM((1024, 256), f32),
            pltpu.VMEM((1024, 256), f32),
            pltpu.VMEM((128, 256), f32),
            pltpu.VMEM((256, 8), f32),
            pltpu.VMEM((1024, 8), f32),
            pltpu.VMEM((256, 128), bf16),
            pltpu.VMEM((1024, 256), bf16),
            pltpu.VMEM((256, 1024), bf16),
            pltpu.VMEM((3, 256, 256), bf16),
            pltpu.VMEM((5, 256, 128), f32),
            pltpu.VMEM((3, 1024, 128), f32),
            pltpu.VMEM((256, 128), f32),
            pltpu.VMEM((1024, BLOCK), bf16),
            pltpu.VMEM((1024, BLOCK), bf16),
            pltpu.VMEM((1024, BLOCK), f32),
            pltpu.VMEM((1024, BLOCK), f32),
            pltpu.VMEM((256, frames), f32),
            pltpu.VMEM((128, frames), f32),
            pltpu.VMEM((256, frames // 2), bf16),
            pltpu.VMEM((256, frames), f32),
            pltpu.VMEM((128, frames), bf16),
            pltpu.SemaphoreType.DMA((5, frames // BLOCK)),
        ],
        compiler_params=PARAMS,
    )(lengths_row, *vecs, *wides, resid_one, attended, cot, wo, we, wr, wd)


def mish_parts(values):
    grown = jnp.exp(jnp.minimum(values, 20.0))
    top = grown * (grown + 2.0)
    inverse = 1.0 / (top + 2.0)
    return (grown, top * inverse, inverse)


def mish_value(values):
    return values * mish_parts(values)[1]


def mish_slope(values):
    grown, ratio, inverse = mish_parts(values)
    return ratio + values * (4.0 * grown * (grown + 1.0)) * (inverse * inverse)


def segment_rows(places, lens_ref, segs):
    segment = segment_of(places, lens_ref, segs)
    row = lax.broadcasted_iota(jnp.int32, (128, places.shape[1]), 0)
    return ((row == segment) & (row < segs)).astype(jnp.float32).astype(jnp.bfloat16)


def stack_parts(values):
    top, mid, last = split_three(values)
    return jnp.concatenate(
        [top.astype(jnp.float32), mid.astype(jnp.float32), last.astype(jnp.float32)], axis=0
    ).astype(jnp.bfloat16)


def unstack_parts(stacked):
    return stacked[0:8] + stacked[8:16] + stacked[16:24]


def segment_totals(rows, hot):
    return unstack_parts(dot_nt(stack_parts(rows), hot))


def segment_values(stat, hot):
    return unstack_parts(dot(stack_parts(stat), hot))


def two_parts(values):
    top = values.astype(jnp.bfloat16)
    return (top, (values - top.astype(jnp.float32)).astype(jnp.bfloat16))


def segment_counts(lens_ref, segs):
    lane = lax.broadcasted_iota(jnp.int32, (8, 128), 1)
    counts = jnp.ones((8, 128), jnp.float32)
    for index in range(segs):
        counts = jnp.where(lane == index, lens_ref[index].astype(jnp.float32), counts)
    return counts


def conv_rows(padded_ref, first, prev, succ):
    width = prev.shape[1]
    wide = padded_ref[:, pl.ds(first, width + 256)].astype(jnp.float32)
    before = pltpu.roll(wide, 1, 1)[:, 128 : 128 + width] * prev
    after = pltpu.roll(wide, width + 255, 1)[:, 128 : 128 + width] * succ
    here = padded_ref[:, pl.ds(pl.multiple_of(first + 128, 128), width)]
    return (before.astype(jnp.bfloat16), here, after.astype(jnp.bfloat16))


def clear_pads(padded_ref):
    rows, width = padded_ref.shape
    padded_ref[:, 0:128] = jnp.zeros((rows, 128), padded_ref.dtype)
    padded_ref[:, width - 128 : width] = jnp.zeros((rows, 128), padded_ref.dtype)


def group_slice(group):
    return slice(32 * group, 32 * group + 32)


def stats_start(stat_ref):
    stat_ref[...] = jnp.zeros_like(stat_ref)


def stats_block(values_of, hot, stat_ref):
    folded = jnp.concatenate(
        [jnp.sum(values_of(group), axis=0, keepdims=True) for group in range(GROUPS)], axis=0
    )
    here = dot_nt(jnp.ones((16, hot.shape[1]), jnp.bfloat16), hot)[0:8]
    mean_here = segment_totals(folded, hot) / jnp.maximum(here * 32.0, 1.0)
    spread = segment_values(mean_here, hot)
    squares = []
    for group in range(GROUPS):
        centered = values_of(group) - spread[group : group + 1]
        squares.append(jnp.sum(centered * centered, axis=0, keepdims=True))
    squares_here = segment_totals(jnp.concatenate(squares, axis=0), hot)
    count, mean, total = stat_ref[0], stat_ref[1], stat_ref[2]
    share = here / jnp.maximum(count + here, 1.0)
    change = mean_here - mean
    stat_ref[0] = count + here
    stat_ref[1] = mean + change * share
    stat_ref[2] = total + squares_here + change * change * (count * 32.0) * share


def stats_scale(stat_ref):
    return lax.rsqrt(stat_ref[2] / jnp.maximum(stat_ref[0] * 32.0, 1.0) + EPSILON)


def halves_down(rows):
    width = rows.shape[1] // 2
    return jnp.concatenate([rows[:, 0:width], rows[:, width:]], axis=0)


def time_low_of(time_ref):
    embedded = time_ref[...].astype(jnp.float32)
    rows = mish_value(embedded).astype(jnp.bfloat16).astype(jnp.float32)
    return jnp.concatenate([rows, jnp.zeros_like(rows)], axis=0)


MESH_ID = pl.DeviceIdType.MESH


class Places:
    def __init__(self, utts, times):
        self.near, self.far, self.group = plane_of(utts, times)
        self.times = times
        self.devices = utts * times
        self.u = lax.axis_index("utt")
        self.t = lax.axis_index("tm")
        self.core = self.u % 2
        self.x = self.u // 2 % self.near
        self.z = self.u // 2 // self.near
        self.member = (self.x * times + self.t) * 2 + self.core

    def plane_peer(self, step):
        other = (self.member + step) % self.group
        rest = other // 2
        return ((self.z * self.near + rest // self.times) * 2 + other % 2, rest % self.times)

    def partner(self):
        return (self.u + 1 - 2 * self.core, self.t)

    def core_peer(self, step):
        other = (self.member // 2 + step) % (self.group // 2)
        return ((self.z * self.near + other // self.times) * 2 + self.core, other % self.times)

    def line_peer(self, step):
        return (((self.z + step) % self.far * self.near + self.x) * 2 + self.core, self.t)

    def greet(self, everyone):
        barrier = pltpu.get_barrier_semaphore()
        if everyone and self.devices <= 64:
            here = self.u * self.times + self.t
            others = [(here + step) % self.devices for step in range(1, self.devices)]
            peers = [(other // self.times, other % self.times) for other in others]
        else:
            peers = [self.plane_peer(step) for step in range(1, self.group)]
            peers += [self.line_peer(step) for step in range(1, self.far)]
        for peer in peers:
            pl.semaphore_signal(barrier, inc=1, device_id=peer, device_id_type=MESH_ID)
        pl.semaphore_wait(barrier, len(peers))


def aligned_rows(at, count):
    return pl.ds(pl.multiple_of(at, 16), count)


class Sender:
    def __init__(self, send_sem, recv_sem):
        self.send_sem, self.recv_sem = send_sem, recv_sem
        self.slot = 0
        self.copies = []

    def send(self, source, target, peer):
        copy = pltpu.make_async_remote_copy(
            src_ref=source,
            dst_ref=target,
            send_sem=self.send_sem.at[self.slot],
            recv_sem=self.recv_sem.at[self.slot],
            device_id=peer,
            device_id_type=MESH_ID,
        )
        copy.start()
        self.slot += 1
        self.copies.append(copy)

    def settle(self):
        for copy in self.copies:
            copy.wait()
        self.copies = []


def copy_semaphores(count):
    return [pltpu.SemaphoreType.DMA((count,)), pltpu.SemaphoreType.DMA((count,))]


def sum_scratch(utts, times, rows):
    near, far, group = plane_of(utts, times)
    part = rows // group
    return [
        pltpu.VMEM((group - 1, part, 256), jnp.bfloat16),
        pltpu.VMEM((part, 256), jnp.bfloat16),
        pltpu.VMEM((far - 1, part // far, 256), jnp.bfloat16),
    ] + copy_semaphores(2 * (group - 1) + 2 * (far - 1))


def sum_stages(places, pack_ref, out_ref, recv_a, sum_a, recv_b, send_sem, recv_sem):
    part, piece = sum_a.shape[0], recv_b.shape[1]
    group, far = places.group, places.far
    base = places.member * part
    sender = Sender(send_sem, recv_sem)

    def in_plane():
        for step in range(1, group):
            other = (places.member + step) % group
            sender.send(pack_ref.at[aligned_rows(other * part, part)], recv_a.at[step - 1], places.plane_peer(step))

    def on_line():
        sender.settle()
        total = pack_ref[aligned_rows(base, part), :].astype(jnp.float32)
        for step in range(1, group):
            total = total + recv_a[step - 1].astype(jnp.float32)
        sum_a[...] = total.astype(jnp.bfloat16)
        for step in range(1, far):
            other = (places.z + step) % far
            sender.send(sum_a.at[aligned_rows(other * piece, piece)], recv_b.at[step - 1], places.line_peer(step))

    def line_back():
        sender.settle()
        total = sum_a[aligned_rows(places.z * piece, piece), :].astype(jnp.float32)
        for step in range(1, far):
            total = total + recv_b[step - 1].astype(jnp.float32)
        mine = aligned_rows(base + places.z * piece, piece)
        out_ref[mine, :] = total.astype(jnp.bfloat16)
        for step in range(1, far):
            sender.send(out_ref.at[mine], out_ref.at[mine], places.line_peer(step))

    def plane_back():
        sender.settle()
        mine = aligned_rows(base, part)
        for step in range(1, group):
            sender.send(out_ref.at[mine], out_ref.at[mine], places.plane_peer(step))

    return [in_plane, on_line, line_back, plane_back, sender.settle]


def direct_scratch(utts, times, rows):
    devices = utts * times
    return [pltpu.VMEM((devices - 1, rows // devices, 256), jnp.bfloat16)] + copy_semaphores(2 * (devices - 1))


def direct_sum_stages(places, pack_ref, out_ref, recv_a, send_sem, recv_sem):
    devices = recv_a.shape[0] + 1
    piece = pack_ref.shape[0] // devices
    times = places.times
    here = places.u * times + places.t
    sender = Sender(send_sem, recv_sem)

    def to_all():
        for step in range(1, devices):
            other = (here + step) % devices
            peer = (other // times, other % times)
            sender.send(pack_ref.at[aligned_rows(other * piece, piece)], recv_a.at[step - 1], peer)

    def back():
        sender.settle()
        mine = aligned_rows(here * piece, piece)
        total = pack_ref[mine, :].astype(jnp.float32)
        for step in range(1, devices):
            total = total + recv_a[step - 1].astype(jnp.float32)
        out_ref[mine, :] = total.astype(jnp.bfloat16)
        for step in range(1, devices):
            other = (here + step) % devices
            sender.send(out_ref.at[mine], out_ref.at[mine], (other // times, other % times))

    def nothing():
        pass

    return [to_all, back, nothing, nothing, sender.settle]


def late_scratch(utts, times, rows):
    return (direct_scratch if utts * times <= 64 else sum_scratch)(utts, times, rows)


def late_stages(places, *refs):
    return (direct_sum_stages if places.devices <= 64 else sum_stages)(places, *refs)


def large_scratch(utts, times, rows):
    near, far, group = plane_of(utts, times)
    chips = group // 2
    half = rows // 2
    part = half // chips
    return [
        pltpu.VMEM((half, 256), jnp.bfloat16),
        pltpu.VMEM((half, 256), jnp.bfloat16),
        pltpu.VMEM((chips - 1, part, 256), jnp.bfloat16),
        pltpu.VMEM((part, 256), jnp.bfloat16),
        pltpu.VMEM((far - 1, part // far, 256), jnp.bfloat16),
    ] + copy_semaphores(2 * (1 + chips - 1 + far - 1))


def large_sum_stages(places, pack_ref, out_ref, recv_a, sum_a, recv_b, sum_b, recv_c, send_sem, recv_sem):
    half, part, piece = sum_a.shape[0], sum_b.shape[0], recv_c.shape[1]
    chips, far, core = places.group // 2, places.far, places.core
    spot = places.member // 2
    base = core * half + spot * part
    sender = Sender(send_sem, recv_sem)

    def between_cores():
        sender.send(pack_ref.at[aligned_rows((1 - core) * half, half)], recv_a, places.partner())

    def in_plane():
        sender.settle()
        own = pack_ref[aligned_rows(core * half, half), :].astype(jnp.float32)
        sum_a[...] = (own + recv_a[...].astype(jnp.float32)).astype(jnp.bfloat16)
        for step in range(1, chips):
            other = (spot + step) % chips
            sender.send(sum_a.at[aligned_rows(other * part, part)], recv_b.at[step - 1], places.core_peer(step))

    def on_line():
        sender.settle()
        total = sum_a[aligned_rows(spot * part, part), :].astype(jnp.float32)
        for step in range(1, chips):
            total = total + recv_b[step - 1].astype(jnp.float32)
        sum_b[...] = total.astype(jnp.bfloat16)
        for step in range(1, far):
            other = (places.z + step) % far
            sender.send(sum_b.at[aligned_rows(other * piece, piece)], recv_c.at[step - 1], places.line_peer(step))

    def line_back():
        sender.settle()
        total = sum_b[aligned_rows(places.z * piece, piece), :].astype(jnp.float32)
        for step in range(1, far):
            total = total + recv_c[step - 1].astype(jnp.float32)
        mine = aligned_rows(base + places.z * piece, piece)
        out_ref[mine, :] = total.astype(jnp.bfloat16)
        for step in range(1, far):
            sender.send(out_ref.at[mine], out_ref.at[mine], places.line_peer(step))

    def plane_back():
        sender.settle()
        mine = aligned_rows(base, part)
        for step in range(1, chips):
            sender.send(out_ref.at[mine], out_ref.at[mine], places.core_peer(step))

    def cores_back():
        sender.settle()
        mine = aligned_rows(core * half, half)
        sender.send(out_ref.at[mine], out_ref.at[mine], places.partner())

    return [between_cores, in_plane, on_line, line_back, plane_back, cores_back, sender.settle]


def chunk_scratch(utts, times, rows):
    near, far, group = plane_of(utts, times)
    part = rows // group
    return [
        pltpu.VMEM((2 * part, 256), jnp.bfloat16),
        pltpu.VMEM((part, 256), jnp.bfloat16),
        pltpu.VMEM((part, 256), jnp.bfloat16),
        pltpu.VMEM((far - 1, part // far, 256), jnp.bfloat16),
    ] + copy_semaphores(1 + 2 * (far - 1) + group // 2 - 1 + 1)


def chunk_sum_stages(places, chunk_refs, out_ref, sum_chips, recv_a, sum_a, recv_b, send_sem, recv_sem):
    part, piece = sum_a.shape[0], recv_b.shape[1]
    chips, far, core = places.group // 2, places.far, places.core
    spot = places.member // 2
    base = (core * chips + spot) * part
    sender = Sender(send_sem, recv_sem)

    def between_cores():
        total = chunk_refs[0][...].astype(jnp.float32)
        for ref in chunk_refs[1:]:
            total = total + ref[...].astype(jnp.float32)
        sum_chips[...] = total.astype(jnp.bfloat16)
        sender.send(sum_chips.at[aligned_rows((1 - core) * part, part)], recv_a, places.partner())

    def on_line():
        sender.settle()
        own = sum_chips[aligned_rows(core * part, part), :].astype(jnp.float32)
        sum_a[...] = (own + recv_a[...].astype(jnp.float32)).astype(jnp.bfloat16)
        for step in range(1, far):
            other = (places.z + step) % far
            sender.send(sum_a.at[aligned_rows(other * piece, piece)], recv_b.at[step - 1], places.line_peer(step))

    def line_back():
        sender.settle()
        total = sum_a[aligned_rows(places.z * piece, piece), :].astype(jnp.float32)
        for step in range(1, far):
            total = total + recv_b[step - 1].astype(jnp.float32)
        mine = aligned_rows(base + places.z * piece, piece)
        out_ref[mine, :] = total.astype(jnp.bfloat16)
        for step in range(1, far):
            sender.send(out_ref.at[mine], out_ref.at[mine], places.line_peer(step))

    def plane_back():
        sender.settle()
        mine = aligned_rows(base, part)
        for step in range(1, chips):
            sender.send(out_ref.at[mine], out_ref.at[mine], places.core_peer(step))

    def cores_back():
        sender.settle()
        mine = aligned_rows(core * chips * part, chips * part)
        sender.send(out_ref.at[mine], out_ref.at[mine], places.partner())

    return [between_cores, on_line, line_back, plane_back, cores_back, sender.settle]


def gather_stages(places, rows_of, own_ref, out_ref, own_sem, send_sem, recv_sem):
    chips, far = places.group // 2, places.far
    spot = places.member // 2
    sender = Sender(send_sem, recv_sem)
    local = []

    def on_line():
        mine = aligned_rows(((places.core * chips + spot) * far + places.z) * 16, 16)
        own_ref[...] = rows_of()
        copy = pltpu.make_async_copy(own_ref, out_ref.at[mine], own_sem.at[0])
        copy.start()
        local.append(copy)
        for step in range(1, far):
            sender.send(own_ref, out_ref.at[mine], places.line_peer(step))

    def in_plane():
        local[0].wait()
        sender.settle()
        mine = aligned_rows((places.core * chips + spot) * far * 16, far * 16)
        for step in range(1, chips):
            sender.send(out_ref.at[mine], out_ref.at[mine], places.core_peer(step))

    def between_cores():
        sender.settle()
        mine = aligned_rows(places.core * chips * far * 16, chips * far * 16)
        sender.send(out_ref.at[mine], out_ref.at[mine], places.partner())

    return [on_line, in_plane, between_cores, sender.settle]


def gather_scratch(utts, times, width):
    near, far, group = plane_of(utts, times)
    return [
        pltpu.VMEM((16, width), jnp.bfloat16),
        pltpu.SemaphoreType.DMA((1,)),
    ] + copy_semaphores(group // 2 - 1 + far - 1 + 1)


def res_forward_kernel(
    segs,
    utts,
    times,
    lens_ref,
    *refs,
):
    vecs = refs[0:10]
    res_forward_body(segs, utts, times, lens_ref, vecs, *refs[10:])


def res_forward_body(
    segs,
    utts,
    times,
    lens_ref,
    vecs,
    noisy_ref,
    mean_ref,
    time_ref,
    wc1_ref,
    tw_ref,
    wc2_ref,
    wsk_ref,
    wh_ref,
    hat_one_hbm,
    act_hbm,
    hat_two_hbm,
    hat_norm_hbm,
    scale_norm_ref,
    resid_hbm,
    proj_hbm,
    scales_ref,
    xin_hbm,
    time_all_ref,
    cols_ref,
    wc1_t,
    wc2_t,
    wsk_t,
    wh_t,
    pre_ref,
    stat_ref,
    time_cols_ref,
    mean_all_ref,
    hat_one_ref,
    act_ref,
    hat_two_ref,
    hat_norm_ref,
    resid_ref,
    proj_ref,
    xin_ref,
    store_sem,
    send_mean,
    arrive_mean,
    *gather_refs,
):
    frames = noisy_ref.shape[1]
    blocks = frames // RES_BLOCK
    stores = (
        (hat_one_ref, hat_one_hbm), (act_ref.at[:, 128 : 128 + frames], act_hbm), (hat_two_ref, hat_two_hbm),
        (hat_norm_ref, hat_norm_hbm), (resid_ref, resid_hbm), (proj_ref, proj_hbm),
        (xin_ref.at[:, 128 : 128 + frames], xin_hbm),
    )

    def store(which, index):
        source, target = stores[which]
        lanes = block_lanes(index, RES_BLOCK)
        return pltpu.make_async_copy(source.at[:, lanes], target.at[:, lanes], store_sem.at[which, index])

    spots = Places(utts, times)
    embedded = gather_stages(
        spots, lambda: halves_down(time_low_of(time_ref)[0:8]).astype(jnp.bfloat16),
        gather_refs[0], time_all_ref, *gather_refs[1:4]
    )
    means = Sender(send_mean, arrive_mean)
    width = frames // times
    spots.greet(False)
    own_lanes = pl.ds(pl.multiple_of(spots.t * width, 128), width)
    for step in range(1, times):
        means.send(mean_ref, mean_all_ref.at[:, own_lanes], (spots.u, (spots.t + step) % times))
    mean_all_ref[:, own_lanes] = mean_ref[...]
    embedded[0]()
    vector_columns(vecs, cols_ref)
    for tap in range(3):
        columns = wc1_ref[tap].astype(jnp.float32).T.astype(jnp.bfloat16)
        wc1_t[0, :, 80 * tap : 80 * tap + 80] = columns[:, 0:80]
        wc1_t[1, :, 80 * tap : 80 * tap + 80] = columns[:, 80:160]
        wc2_t[:, 256 * tap : 256 * tap + 256] = wc2_ref[tap].T
    wsk_t[...] = wsk_ref[...].astype(jnp.float32).T.astype(jnp.bfloat16)
    wh_t[...] = wh_ref[...].T
    time_rows = dot(time_low_of(time_ref).astype(jnp.bfloat16), tw_ref[...]) + vector_row(vecs[3])
    seg_row = lax.broadcasted_iota(jnp.int32, (16, 256), 0)
    time_rows = jnp.where(seg_row < segs, time_rows, 0.0)
    time_cols = jnp.concatenate([time_rows, jnp.zeros((112, 256), jnp.float32)], axis=0).T
    time_top, time_mid = two_parts(time_cols)
    time_cols_ref[:, 0:128] = time_top
    time_cols_ref[:, 128:256] = time_mid
    clear_pads(xin_ref)
    clear_pads(act_ref)

    def column(index):
        return cols_ref[:, index : index + 1]

    def input_phase(source_ref, row):
        def step(index, carry):
            first = pl.multiple_of(index * RES_BLOCK, RES_BLOCK)
            valid, _, _ = frame_masks(places_of(first, RES_BLOCK), lens_ref, segs)
            rows = source_ref[:, pl.ds(first, RES_BLOCK)].astype(jnp.float32) * valid
            here = pl.ds(pl.multiple_of(first + 128, 128), RES_BLOCK)
            xin_ref[row : row + 80, here] = rows.astype(jnp.bfloat16)
            return carry

        lax.fori_loop(0, blocks, step, 0)

    def taps_of(padded_ref, index):
        first = pl.multiple_of(index * RES_BLOCK, RES_BLOCK)
        places = places_of(first, RES_BLOCK)
        _, prev, succ = frame_masks(places, lens_ref, segs)
        return (first, places, jnp.concatenate(conv_rows(padded_ref, first, prev, succ), axis=0))

    def conv_phase(padded_ref, weight, start_of):
        stats_start(stat_ref)

        def step(index, carry):
            first, places, taps = taps_of(padded_ref, index)
            pre_ref[:, pl.ds(first, RES_BLOCK)] = dot(weight[...], taps) + start_of(first)
            stats_block(
                lambda group: pre_ref[group_slice(group), pl.ds(first, RES_BLOCK)],
                segment_rows(places, lens_ref, segs),
                stat_ref,
            )
            return carry

        lax.fori_loop(0, blocks, step, 0)

    def noisy_step(index, carry):
        first, _, taps = taps_of(xin_ref.at[0:80], index)
        pre_ref[:, pl.ds(first, RES_BLOCK)] = dot(wc1_t[0], taps) + column(0)
        return carry

    input_phase(noisy_ref, 0)
    lax.fori_loop(0, blocks, noisy_step, 0)
    means.settle()
    embedded[1]()
    input_phase(mean_all_ref, 80)
    conv_phase(xin_ref.at[80:160], wc1_t.at[1], lambda first: pre_ref[:, pl.ds(first, RES_BLOCK)])
    for index in range(blocks):
        store(6, index).start()
    embedded[2]()
    scales_ref[0] = stats_scale(stat_ref)

    def act_step(index, carry):
        first = pl.multiple_of(index * RES_BLOCK, RES_BLOCK)
        places = places_of(first, RES_BLOCK)
        valid, _, _ = frame_masks(places, lens_ref, segs)
        hot = segment_rows(places, lens_ref, segs)
        mean = segment_values(stat_ref[1], hot)
        scale = segment_values(scales_ref[0], hot)
        timed = dot(time_cols_ref[...], jnp.concatenate([hot, hot], axis=0))
        for group in range(GROUPS):
            rows = group_slice(group)
            hat = (pre_ref[rows, pl.ds(first, RES_BLOCK)] - mean[group : group + 1]) * scale[group : group + 1]
            hat_one_ref[rows, pl.ds(first, RES_BLOCK)] = hat.astype(jnp.bfloat16)
            value = mish_value(hat * cols_ref[rows, 1:2] + cols_ref[rows, 2:3]) + timed[rows]
            act_ref[rows, pl.ds(pl.multiple_of(first + 128, 128), RES_BLOCK)] = (value * valid).astype(jnp.bfloat16)
        store(0, index).start()
        store(1, index).start()
        return carry

    lax.fori_loop(0, blocks, act_step, 0)
    conv_phase(act_ref, wc2_t, lambda first: column(4))
    embedded[3]()
    scales_ref[1] = stats_scale(stat_ref)

    def resid_step(index, carry):
        first = pl.multiple_of(index * RES_BLOCK, RES_BLOCK)
        places = places_of(first, RES_BLOCK)
        valid, _, _ = frame_masks(places, lens_ref, segs)
        hot = segment_rows(places, lens_ref, segs)
        mean = segment_values(stat_ref[1], hot)
        scale = segment_values(scales_ref[1], hot)
        skip = dot(wsk_t[...], xin_ref[:, pl.ds(pl.multiple_of(first + 128, 128), RES_BLOCK)])
        for group in range(GROUPS):
            rows = group_slice(group)
            hat = (pre_ref[rows, pl.ds(first, RES_BLOCK)] - mean[group : group + 1]) * scale[group : group + 1]
            hat_two_ref[rows, pl.ds(first, RES_BLOCK)] = hat.astype(jnp.bfloat16)
            value = mish_value(hat * cols_ref[rows, 5:6] + cols_ref[rows, 6:7]) * valid
            resid_ref[rows, pl.ds(first, RES_BLOCK)] = value + skip[rows] + cols_ref[rows, 7:8]
        hat, scale = norm_frames(resid_ref[:, pl.ds(first, RES_BLOCK)])
        hat_norm_ref[:, pl.ds(first, RES_BLOCK)] = hat.astype(jnp.bfloat16)
        scale_norm_ref[:, pl.ds(first, RES_BLOCK)] = jnp.broadcast_to(scale, (8, RES_BLOCK))
        normed = (hat * column(8) + column(9)).astype(jnp.bfloat16)
        proj_ref[:, pl.ds(first, RES_BLOCK)] = dot(wh_t[...], normed).astype(jnp.bfloat16)
        for which in range(2, 6):
            store(which, index).start()
        return carry

    lax.fori_loop(0, blocks, resid_step, 0)
    for which in range(7):
        for index in range(blocks):
            store(which, index).wait()


def res_forward(utts, times, lengths_row, vecs, noisy, mean, embedded, wc1, tw, wc2, wsk, wh):
    frames = noisy.shape[1]
    f32 = jnp.float32
    bf16 = jnp.bfloat16
    return pl.pallas_call(
        functools.partial(res_forward_kernel, lengths_row.shape[0], utts, times),
        name="res_forward",
        out_shape=(
            jax.ShapeDtypeStruct((256, frames), bf16),
            jax.ShapeDtypeStruct((256, frames), bf16),
            jax.ShapeDtypeStruct((256, frames), bf16),
            jax.ShapeDtypeStruct((256, frames), bf16),
            jax.ShapeDtypeStruct((8, frames), f32),
            jax.ShapeDtypeStruct((256, frames), f32),
            jax.ShapeDtypeStruct((384, frames), bf16),
            jax.ShapeDtypeStruct((2, 8, 128), f32),
            jax.ShapeDtypeStruct((160, frames), bf16),
            jax.ShapeDtypeStruct((utts * times * 16, embedded.shape[1] // 2), bf16),
        ),
        in_specs=[SCALARS] + [WHOLE] * 18,
        out_specs=(ANYWHERE,) * 4 + (WHOLE,) + (ANYWHERE,) * 2 + (WHOLE,) + (ANYWHERE,) * 2,
        scratch_shapes=[
            pltpu.VMEM((256, 16), f32),
            pltpu.VMEM((2, 256, 240), bf16),
            pltpu.VMEM((256, 768), bf16),
            pltpu.VMEM((256, 160), bf16),
            pltpu.VMEM((384, 256), bf16),
            pltpu.VMEM((256, frames), f32),
            pltpu.VMEM((3, 8, 128), f32),
            pltpu.VMEM((256, 256), bf16),
            pltpu.VMEM((80, frames), bf16),
            pltpu.VMEM((256, frames), bf16),
            pltpu.VMEM((256, frames + 256), bf16),
            pltpu.VMEM((256, frames), bf16),
            pltpu.VMEM((256, frames), bf16),
            pltpu.VMEM((256, frames), f32),
            pltpu.VMEM((384, frames), bf16),
            pltpu.VMEM((160, frames + 256), bf16),
            pltpu.SemaphoreType.DMA((7, frames // RES_BLOCK)),
        ]
        + copy_semaphores(times - 1)
        + gather_scratch(utts, times, embedded.shape[1] // 2),
        compiler_params=pltpu.CompilerParams(
            vmem_limit_bytes=VMEM_LIMIT, collective_id=0, has_side_effects=True
        ),
    )(lengths_row, *vecs, noisy, mean, embedded, wc1, tw, wc2, wsk, wh)


def norm_back_sums(grad_of, hat_ref, gain_index, shift_index, first, hot, cols_ref, dhat_ref, part_ref, part_at, stat_ref):
    ones = []
    twos = []
    for group in range(GROUPS):
        rows = group_slice(group)
        hat = hat_ref[rows, pl.ds(first, RES_BLOCK)].astype(jnp.float32)
        gain = cols_ref[rows, gain_index : gain_index + 1]
        slope = mish_slope(hat * gain + cols_ref[rows, shift_index : shift_index + 1])
        grad = grad_of(rows) * slope
        part_ref[part_at, rows, :] += lane_fold(grad * hat)
        part_ref[part_at + 1, rows, :] += lane_fold(grad)
        grad_hat = grad * gain
        dhat_ref[rows, pl.ds(first, RES_BLOCK)] = grad_hat
        ones.append(jnp.sum(grad_hat, axis=0, keepdims=True))
        twos.append(jnp.sum(grad_hat * hat, axis=0, keepdims=True))
    stat_ref[0] += segment_totals(jnp.concatenate(ones, axis=0), hot)
    stat_ref[1] += segment_totals(jnp.concatenate(twos, axis=0), hot)


def norm_back_apply(hat_ref, scale_stat, first, hot, counts, dhat_ref, stat_ref, padded_ref, part_ref, part_at):
    mean_one = segment_values(stat_ref[0] / (counts * 32.0), hot)
    mean_two = segment_values(stat_ref[1] / (counts * 32.0), hot)
    scale = segment_values(scale_stat, hot)
    for group in range(GROUPS):
        rows = group_slice(group)
        at = slice(group, group + 1)
        hat = hat_ref[rows, pl.ds(first, RES_BLOCK)].astype(jnp.float32)
        grad = scale[at] * (dhat_ref[rows, pl.ds(first, RES_BLOCK)] - mean_one[at] - hat * mean_two[at])
        part_ref[part_at, rows, :] += lane_fold(grad)
        padded_ref[rows, pl.ds(pl.multiple_of(first + 128, 128), RES_BLOCK)] = grad.astype(jnp.bfloat16)


def res_backward_kernel(segs, utts, times, lens_ref, *refs):
    chunks = 10 + plane_of(utts, times)[2] // 2
    res_backward_body(segs, utts, times, lens_ref, refs[0:10], refs[10:chunks], *refs[chunks:])


def res_backward_body(
    segs,
    utts,
    times,
    lens_ref,
    vecs,
    tail_refs,
    gtwo_hbm,
    gproj_hbm,
    hat_norm_hbm,
    scale_norm_ref,
    hat_two_hbm,
    act_hbm,
    hat_one_hbm,
    scales_ref,
    xin_hbm,
    time_ref,
    wc1_ref,
    tw_ref,
    wc2_ref,
    wsk_ref,
    wh_ref,
    gnoisy_hbm,
    gmean_out_ref,
    gtime_ref,
    early_out,
    middle_out,
    late_out,
    tail_out,
    gseg_all_ref,
    cols_ref,
    wc1_b,
    wc2_b,
    gsk_ref,
    dhat_ref,
    gpre_ref,
    part_ref,
    stat_ref,
    gwh_ref,
    gwsk_ref,
    gwc2_ref,
    gwc1_ref,
    gseg_ref,
    gtwo_ref,
    gproj_ref,
    hat_norm_ref,
    hat_two_ref,
    act_ref,
    hat_one_ref,
    xin_ref,
    gnoisy_ref,
    load_sem,
    store_sem,
    gmean_ref,
    recv_mean,
    early_ref,
    middle_ref,
    late_ref,
    *stream_refs,
):
    frames = gtwo_ref.shape[1]
    blocks = frames // RES_BLOCK
    blocked = (
        (gproj_hbm, gproj_ref), (hat_norm_hbm, hat_norm_ref), (gtwo_hbm, gtwo_ref), (hat_two_hbm, hat_two_ref),
        (xin_hbm, xin_ref), (act_hbm, act_ref), (hat_one_hbm, hat_one_ref),
    )

    def load(which, index):
        source, target = blocked[which]
        lanes = block_lanes(index, RES_BLOCK)
        return pltpu.make_async_copy(source.at[:, lanes], target.at[:, lanes], load_sem.at[which, index])

    def store(index):
        lanes = block_lanes(index, BLOCK)
        return pltpu.make_async_copy(gnoisy_ref.at[:, lanes], gnoisy_hbm.at[:, lanes], store_sem.at[index])

    for index in range(blocks):
        for which in range(5):
            load(which, index).start()
    for which in range(5, 7):
        for index in range(blocks):
            load(which, index).start()
    spots = Places(utts, times)
    late_end = 10 + len(late_scratch(utts, times, late_ref.shape[0]))
    rest_refs = stream_refs[late_end:]
    early = sum_stages(spots, early_ref, early_out, *stream_refs[0:5])
    middle = sum_stages(spots, middle_ref, middle_out, *stream_refs[5:10])
    late = late_stages(spots, late_ref, late_out, *stream_refs[10:late_end])
    segments = gather_stages(
        spots, lambda: halves_down(gseg_ref[...].T[0:8]).astype(jnp.bfloat16),
        rest_refs[0], gseg_all_ref, *rest_refs[1:4]
    )
    means = Sender(*rest_refs[4:6])
    tail = chunk_sum_stages(spots, tail_refs, tail_out, *rest_refs[6:12])
    spots.greet(True)
    tail[0]()
    vector_columns(vecs, cols_ref)
    for tap in range(3):
        wc1_b[:, 256 * tap : 256 * tap + 256] = wc1_ref[tap]
        wc2_b[:, 256 * tap : 256 * tap + 256] = wc2_ref[tap]
    for ref in (part_ref, stat_ref, gwh_ref, gwsk_ref, gwc2_ref, gwc1_ref, gseg_ref):
        ref[...] = jnp.zeros_like(ref)
    clear_pads(gpre_ref)
    counts = segment_counts(lens_ref, segs)

    def column(index):
        return cols_ref[:, index : index + 1]

    def layout(index):
        first = pl.multiple_of(index * RES_BLOCK, RES_BLOCK)
        places = places_of(first, RES_BLOCK)
        return (first, places, frame_masks(places, lens_ref, segs))

    def project_step(index, carry):
        for which in range(5):
            load(which, index).wait()
        first, places, (valid, _, _) = layout(index)
        hot = segment_rows(places, lens_ref, segs)
        gproj = gproj_ref[:, pl.ds(first, RES_BLOCK)]
        g_normed = dot(wh_ref[...], gproj)
        hat = hat_norm_ref[:, pl.ds(first, RES_BLOCK)].astype(jnp.float32)
        normed = (hat * column(8) + column(9)).astype(jnp.bfloat16)
        gwh_ref[...] += dot_nt(gproj, normed)
        part_ref[0] += lane_fold(g_normed * hat)
        part_ref[1] += lane_fold(g_normed)
        back = norm_frames_back(g_normed * column(8), hat, scale_norm_ref[0:1, pl.ds(first, RES_BLOCK)])
        dhat_ref[:, pl.ds(first, RES_BLOCK)] = gtwo_ref[:, pl.ds(first, RES_BLOCK)] + back
        g_skip = dhat_ref[:, pl.ds(first, RES_BLOCK)].astype(jnp.bfloat16)
        gsk_ref[:, pl.ds(first, RES_BLOCK)] = g_skip
        part_ref[2] += lane_fold(g_skip.astype(jnp.float32))
        gwsk_ref[...] += dot_nt(xin_ref[:, pl.ds(first, RES_BLOCK)], g_skip)
        norm_back_sums(
            lambda rows: dhat_ref[rows, pl.ds(first, RES_BLOCK)] * valid,
            hat_two_ref, 5, 6, first, hot, cols_ref, dhat_ref, part_ref, 3, stat_ref,
        )
        return carry

    lax.fori_loop(0, blocks, project_step, 0)
    tail[1]()
    early_ref[0:384, :] = gwh_ref[...].astype(jnp.bfloat16)
    early_ref[384:512, :] = gwsk_ref[0:128, :].astype(jnp.bfloat16)
    fill_rest(early_ref, 512)
    early[0]()

    def apply_two_step(index, carry):
        first, places, _ = layout(index)
        hot = segment_rows(places, lens_ref, segs)
        norm_back_apply(hat_two_ref, scales_ref[1], first, hot, counts, dhat_ref, stat_ref, gpre_ref, part_ref, 5)
        return carry

    lax.fori_loop(0, blocks, apply_two_step, 0)
    stat_ref[...] = jnp.zeros_like(stat_ref)

    def conv_two_weight_step(index, carry):
        load(5, index).wait()
        load(6, index).wait()
        first, places, (valid, prev, succ) = layout(index)
        taps = jnp.concatenate(conv_rows(gpre_ref, first, prev, succ)[::-1], axis=0)
        gwc2_ref[...] += dot_nt(act_ref[:, pl.ds(first, RES_BLOCK)], taps)
        return carry

    lax.fori_loop(0, blocks, conv_two_weight_step, 0)
    for tap in range(3):
        middle_ref[256 * tap : 256 * tap + 256, :] = gwc2_ref[:, 256 * tap : 256 * tap + 256].astype(jnp.bfloat16)
    middle_ref[768:800, :] = gwsk_ref[128:160, :].astype(jnp.bfloat16)
    fill_rest(middle_ref, 800)
    middle[0]()
    tail[2]()
    early[1]()

    def conv_two_step(index, carry):
        first, places, (valid, prev, succ) = layout(index)
        hot = segment_rows(places, lens_ref, segs)
        before, here, after = conv_rows(gpre_ref, first, prev, succ)
        taps = jnp.concatenate([after, here, before], axis=0)
        dhat_ref[:, pl.ds(first, RES_BLOCK)] = dot(wc2_b[...], taps) * valid
        top, mid = two_parts(dhat_ref[:, pl.ds(first, RES_BLOCK)])
        gseg_ref[...] += dot_nt(top, hot) + dot_nt(mid, hot)
        norm_back_sums(
            lambda rows: dhat_ref[rows, pl.ds(first, RES_BLOCK)],
            hat_one_ref, 1, 2, first, hot, cols_ref, dhat_ref, part_ref, 6, stat_ref,
        )
        return carry

    lax.fori_loop(0, blocks // 2, conv_two_step, 0)
    tail[3]()
    lax.fori_loop(blocks // 2, blocks, conv_two_step, 0)
    segments[0]()
    middle[1]()
    early[2]()

    def apply_one_step(index, carry):
        first, places, _ = layout(index)
        hot = segment_rows(places, lens_ref, segs)
        norm_back_apply(hat_one_ref, scales_ref[0], first, hot, counts, dhat_ref, stat_ref, gpre_ref, part_ref, 8)
        return carry

    lax.fori_loop(0, blocks, apply_one_step, 0)
    segments[1]()
    early[3]()

    def conv_one_step(index, carry):
        first, places, (valid, prev, succ) = layout(index)
        before, here, after = conv_rows(gpre_ref, first, prev, succ)
        taps = jnp.concatenate([after, here, before], axis=0)
        gwc1_ref[...] += dot_nt(xin_ref[:, pl.ds(first, RES_BLOCK)], taps)
        return carry

    lax.fori_loop(0, blocks, conv_one_step, 0)
    for tap in range(3):
        late_ref[160 * tap : 160 * tap + 160, :] = gwc1_ref[:, 256 * tap : 256 * tap + 256].astype(jnp.bfloat16)
    rows = [column_sums(part_ref.at[index]) for index in range(9)]
    rows.append(jnp.zeros((7, 256), jnp.float32))
    late_ref[480:496, :] = jnp.concatenate(rows, axis=0).astype(jnp.bfloat16)
    fill_rest(late_ref, 496)
    late[0]()
    segments[2]()
    middle[2]()

    def inputs_step(index, carry):
        first = pl.multiple_of(index * BLOCK, BLOCK)
        valid, prev, succ = frame_masks(places_of(first, BLOCK), lens_ref, segs)
        taps = jnp.concatenate(conv_rows(gpre_ref, first, prev, succ)[::-1], axis=0)
        g_in = dot(wc1_b[...], taps) + dot(wsk_ref[...], gsk_ref[:, pl.ds(first, BLOCK)])
        g_in = g_in * valid
        gnoisy_ref[:, pl.ds(first, BLOCK)] = g_in[0:80]
        store(index).start()
        gmean_ref[:, pl.ds(first, BLOCK)] = g_in[80:160].astype(jnp.bfloat16)
        return carry

    small_blocks = frames // BLOCK
    width = frames // times
    for step in range(1, times + 1):
        owner = (spots.t + step) % times
        lax.fori_loop(owner * (small_blocks // times), (owner + 1) * (small_blocks // times), inputs_step, 0)
        if step < times:
            lanes = pl.ds(pl.multiple_of(owner * width, 128), width)
            means.send(gmean_ref.at[:, lanes], recv_mean.at[step - 1], (spots.u, owner))
    late[1]()
    middle[3]()
    tail[4]()
    segments[3]()
    early[4]()
    grad_low = dot_nt(gseg_ref[...].T[0:16].astype(jnp.bfloat16), tw_ref[...])
    gtime_ref[...] = grad_low[0:8] * mish_slope(time_ref[...].astype(jnp.float32))
    late[2]()
    means.settle()
    total = gmean_ref[:, pl.ds(pl.multiple_of(spots.t * width, 128), width)].astype(jnp.float32)
    for step in range(1, times):
        total = total + recv_mean[step - 1].astype(jnp.float32)
    gmean_out_ref[...] = total
    late[3]()
    middle[4]()
    tail[5]()
    late[4]()
    for index in range(small_blocks):
        store(index).wait()


def fill_rest(ref, rows):
    if ref.shape[0] > rows:
        ref[rows:, :] = jnp.zeros((ref.shape[0] - rows, ref.shape[1]), ref.dtype)


def padded_rows(rows, utts, times):
    return rows + -rows % (16 * utts * times)


def res_backward(
    utts, times, lengths_row, vecs, gtwo, gproj, hat_norm, scale_norm, hat_two, act, hat_one, scales, xin,
    embedded, wc1, tw, wc2, wsk, wh, tail,
):
    frames = gtwo.shape[1]
    f32 = jnp.float32
    bf16 = jnp.bfloat16
    early, middle, late = (padded_rows(rows, utts, times) for rows in (512, 800, 496))
    devices = utts * times
    tail_rows = tail[0].shape[0] * len(tail)
    return pl.pallas_call(
        functools.partial(res_backward_kernel, lengths_row.shape[0], utts, times),
        name="res_backward",
        out_shape=(
            jax.ShapeDtypeStruct((80, frames), f32),
            jax.ShapeDtypeStruct((80, frames // times), f32),
            jax.ShapeDtypeStruct(embedded.shape, f32),
            jax.ShapeDtypeStruct((early, 256), bf16),
            jax.ShapeDtypeStruct((middle, 256), bf16),
            jax.ShapeDtypeStruct((late, 256), bf16),
            jax.ShapeDtypeStruct((tail_rows, 256), bf16),
            jax.ShapeDtypeStruct((devices * 16, 128), bf16),
        ),
        in_specs=[SCALARS] + [WHOLE] * (10 + len(tail)) + [ANYWHERE] * 3 + [WHOLE] + [ANYWHERE] * 3 + [WHOLE] + [ANYWHERE] + [WHOLE] * 6,
        out_specs=(ANYWHERE,) + (WHOLE,) * 6 + (ANYWHERE,),
        scratch_shapes=[
            pltpu.VMEM((256, 16), f32),
            pltpu.VMEM((160, 768), bf16),
            pltpu.VMEM((256, 768), bf16),
            pltpu.VMEM((256, frames), bf16),
            pltpu.VMEM((256, frames), f32),
            pltpu.VMEM((256, frames + 256), bf16),
            pltpu.VMEM((9, 256, 128), f32),
            pltpu.VMEM((2, 8, 128), f32),
            pltpu.VMEM((384, 256), f32),
            pltpu.VMEM((160, 256), f32),
            pltpu.VMEM((256, 768), f32),
            pltpu.VMEM((160, 768), f32),
            pltpu.VMEM((256, 128), f32),
            pltpu.VMEM((256, frames), f32),
            pltpu.VMEM((384, frames), bf16),
            pltpu.VMEM((256, frames), bf16),
            pltpu.VMEM((256, frames), bf16),
            pltpu.VMEM((256, frames), bf16),
            pltpu.VMEM((256, frames), bf16),
            pltpu.VMEM((160, frames), bf16),
            pltpu.VMEM((80, frames), f32),
            pltpu.SemaphoreType.DMA((7, frames // RES_BLOCK)),
            pltpu.SemaphoreType.DMA((frames // BLOCK,)),
            pltpu.VMEM((80, frames), bf16),
            pltpu.VMEM((times - 1, 80, frames // times), bf16),
            pltpu.VMEM((early, 256), bf16),
            pltpu.VMEM((middle, 256), bf16),
            pltpu.VMEM((late, 256), bf16),
        ]
        + sum_scratch(utts, times, early)
        + sum_scratch(utts, times, middle)
        + late_scratch(utts, times, late)
        + gather_scratch(utts, times, 128)
        + copy_semaphores(times - 1)
        + chunk_scratch(utts, times, tail_rows),
        compiler_params=pltpu.CompilerParams(
            vmem_limit_bytes=VMEM_LIMIT, collective_id=1, has_side_effects=True
        ),
        cost_estimate=pl.CostEstimate(flops=40_000_000_000, bytes_accessed=30_000_000, transcendentals=0),
    )(
        lengths_row, *vecs, *tail, gtwo, gproj, hat_norm, scale_norm, hat_two, act, hat_one, scales, xin, embedded,
        wc1, tw, wc2, wsk, wh,
    )


def unpack_kernel(gnoisy, gmean, gtime, early_ref, middle_ref, late_ref, tail_ref, gseg_all_ref, time_all_ref, *refs):
    count = len(GRAD_SHAPES)
    finals, large, sem = refs[3 : count + 3], refs[count + 3 : -1], refs[-1]
    copies = []

    def send(source, target):
        copies.append(pltpu.make_async_copy(source, target, sem.at[len(copies)]))
        copies[-1].start()

    for source, target in zip((gnoisy, gmean, gtime), refs[0:3]):
        send(source, target)
    staged = dict(zip(LARGE_GRADS, large))
    outs = [staged.get(index, ref) for index, ref in enumerate(finals)]
    (
        gwc1, gb1, gg1, gs1, gtw, gtb, gwc2, gb2, gg2, gs2, gwsk, gsb, gng, gns, gwh, gwo, gob, gfg, gfs, gwe, geb, gsa,
        gsbeta, gwr, grb, gwd, gdb,
    ) = outs
    f32 = jnp.float32
    for tap in range(3):
        gwc1[tap] = late_ref[160 * tap : 160 * tap + 160, :].astype(f32)
        gwc2[tap] = middle_ref[256 * tap : 256 * tap + 256, :].astype(f32)
        gwd[tap] = tail_ref[256 * tap : 256 * tap + 256, :].astype(f32)
    gwh[...] = early_ref[0:384, :].astype(f32).T
    gwsk[0:128, :] = early_ref[384:512, :].astype(f32)
    gwsk[128:160, :] = middle_ref[768:800, :].astype(f32)
    rows = late_ref[480:496, :].astype(f32)
    for at, ref in enumerate((gng, gns, gsb, gg2, gs2, gb2, gg1, gs1, gb1)):
        ref[...] = rows[at : at + 1]
    half = time_all_ref.shape[1]
    time_cols = time_all_ref[...].T
    seg_rows = gseg_all_ref[...].astype(f32)
    low_half = lax.broadcasted_iota(jnp.int32, seg_rows.shape, 0) % 16 < 8
    swapped = jnp.concatenate([seg_rows[8:], seg_rows[0:8]], axis=0)
    behind = jnp.concatenate([seg_rows[-8:], seg_rows[0:-8]], axis=0)
    zero = jnp.zeros_like(seg_rows)
    first = jnp.concatenate([jnp.where(low_half, seg_rows, zero), jnp.where(low_half, swapped, zero)], axis=1)
    second = jnp.concatenate([jnp.where(low_half, zero, behind), jnp.where(low_half, zero, seg_rows)], axis=1)
    gtw[0:half, :] = dot(time_cols, first.astype(jnp.bfloat16))
    gtw[half:, :] = dot(time_cols, second.astype(jnp.bfloat16))
    gtb[...] = jnp.sum(first, axis=0, keepdims=True)
    gwr[...] = tail_ref[768:1792, :].astype(f32)
    for index in (0, 4, 6, 10, 14, 25):
        send(staged[index], finals[index])
    gwe[...] = tail_ref[1792:2816, :].astype(f32).T
    gwo[...] = tail_ref[2816:2944, :].astype(f32)
    for index in (15, 19, 23):
        send(staged[index], finals[index])
    rows = tail_ref[2944:2976, :].astype(f32)
    for at, ref in enumerate((gdb, grb, gfg, gfs, gob)):
        ref[...] = rows[at : at + 1]
    for at, ref in enumerate((geb, gsa, gsbeta)):
        for part in range(4):
            ref[:, 256 * part : 256 * part + 256] = rows[5 + 4 * at + part : 6 + 4 * at + part]
    for copy in copies:
        copy.wait()


GRAD_SHAPES = (
    (3, 160, 256), (1, 256), (1, 256), (1, 256), (1024, 256), (1, 256), (3, 256, 256), (1, 256), (1, 256), (1, 256),
    (160, 256), (1, 256), (1, 256), (1, 256), (256, 384), (128, 256), (1, 256), (1, 256), (1, 256), (256, 1024),
    (1, 1024), (1, 1024), (1, 1024), (1024, 256), (1, 256), (3, 256, 256), (1, 256),
)


LARGE_GRADS = (0, 4, 6, 10, 14, 15, 19, 23, 25)


def unpack_grads(gnoisy, gmean, gtime, *packed):
    carried = tuple(jax.ShapeDtypeStruct(item.shape, item.dtype) for item in (gnoisy, gmean, gtime))
    shapes = tuple(jax.ShapeDtypeStruct(shape, jnp.float32) for shape in GRAD_SHAPES)
    specs = tuple(ANYWHERE if index in LARGE_GRADS else WHOLE for index in range(len(GRAD_SHAPES)))
    outs = pl.pallas_call(
        unpack_kernel,
        name="unpack_grads",
        out_shape=carried + shapes,
        in_specs=[WHOLE] * (3 + len(packed)),
        out_specs=(ANYWHERE,) * 3 + specs,
        scratch_shapes=[pltpu.VMEM(GRAD_SHAPES[index], jnp.float32) for index in LARGE_GRADS]
        + [pltpu.SemaphoreType.DMA((3 + len(LARGE_GRADS),))],
        compiler_params=PARAMS,
    )(gnoisy, gmean, gtime, *packed)
    grads = tuple(out.reshape(out.shape[1]) if out.shape[0] == 1 else out for out in outs[3:])
    return (outs[0][None], outs[1], outs[2][None]) + grads


TAIL_ROWS = 2976


def shards(
    utts,
    times,
    noisy_mel,
    encoder_mean,
    time_embedding,
    utter_lengths,
    out_cotangent,
    conv_one,
    bias_one,
    gain_one,
    shift_one,
    time_weight,
    time_bias,
    conv_two,
    bias_two,
    gain_two,
    shift_two,
    skip_weight,
    skip_bias,
    norm_gain,
    norm_shift,
    heads_input,
    heads_output,
    output_bias,
    feed_gain,
    feed_shift,
    expand_weight,
    expand_bias,
    snake_alpha,
    snake_beta,
    reduce_weight,
    reduce_bias,
    down_weight,
    down_bias,
):
    lengths_row = utter_lengths[0]
    noisy = noisy_mel[0]
    embedded = time_embedding[0]
    vecs_res = (
        bias_one, gain_one, shift_one, time_bias, bias_two, gain_two, shift_two, skip_bias, norm_gain, norm_shift
    )
    hat_one, act, hat_two, hat_norm, scale_norm, resid_one, projected, scales, xin, time_all = res_forward(
        utts, times, lengths_row, vecs_res, noisy, encoder_mean, embedded, conv_one, time_weight, conv_two, skip_weight, heads_input
    )
    attended, log_sums = attention_forward(projected, lengths_row)
    down_output, grad_two, grad_attended, *tail = feed_forward(
        utts, times, padded_rows(TAIL_ROWS, utts, times), lengths_row, (output_bias, feed_gain, feed_shift, reduce_bias, down_bias),
        (expand_bias, snake_alpha, snake_beta), resid_one, attended, out_cotangent[0],
        heads_output, expand_weight, reduce_weight, down_weight,
    )
    tail = tail[0:1] + [
        lax.ppermute(chunk, ("utt", "tm"), chunk_moves(utts, times, step + 1)) for step, chunk in enumerate(tail[1:])
    ]
    grad_projected = attention_backward(projected, attended, log_sums, grad_attended, lengths_row)
    grad_noisy, grad_mean, grad_time, *packed = res_backward(
        utts, times, lengths_row, vecs_res, grad_two, grad_projected, hat_norm, scale_norm, hat_two, act, hat_one,
        scales, xin, embedded, conv_one, time_weight, conv_two, skip_weight, heads_input, tail,
    )
    return (down_output[None],) + unpack_grads(grad_noisy, grad_mean, grad_time, *packed, time_all)


def solution(mesh):
    return jax.shard_map(
        functools.partial(shards, mesh.shape["utt"], mesh.shape["tm"]),
        mesh=mesh,
        in_specs=(
            P("tm", None, "utt"),
            P(None, ("utt", "tm")),
            P("tm", "utt", None),
            P("utt", None),
            P("tm", None, "utt"),
            P(),
            P(),
            P(),
            P(),
            P(),
            P(),
            P(),
            P(),
            P(),
            P(),
            P(),
            P(),
            P(),
            P(),
            P(),
            P(),
            P(),
            P(),
            P(),
            P(),
            P(),
            P(),
            P(),
            P(),
            P(),
            P(),
            P(),
        ),
        out_specs=(
            P("tm", None, "utt"),
            P("tm", None, "utt"),
            P(None, ("utt", "tm")),
            P("tm", "utt", None),
            P(),
            P(),
            P(),
            P(),
            P(),
            P(),
            P(),
            P(),
            P(),
            P(),
            P(),
            P(),
            P(),
            P(),
            P(),
            P(),
            P(),
            P(),
            P(),
            P(),
            P(),
            P(),
            P(),
            P(),
            P(),
            P(),
            P(),
        ),
        check_vma=False,
    )
```
